32 devices in a mesh: dp: 8 (over z, x), mp: 4 (over y, core).
Axes of the slice: x: 2, y: 2, z: 4, core: 2. Of those that a mesh axis runs over, the one named last changes fastest.
Arguments:
- layer_in: bfloat16 [16384, 768], P(('dp', 'mp')), may hold values from -6 to 6
- ln1_gain: float32 [768], replicated, may hold values from 0.5 to 1.5
- ln1_bias: float32 [768], replicated, may hold values from -1.25 to 1.25
- w_qkv: bfloat16 [3, 768, 768], P(None, None, 'mp'), may hold values from -0.21875 to 0.21875
- b_qv: float32 [2, 768], P(None, 'mp'), may hold values from -1.75 to 1.75
- rel_row: float32 [12, 27], P('mp'), may hold values from -3 to 3
- rel_col: float32 [12, 27], P('mp'), may hold values from -3 to 3
- w_out: bfloat16 [768, 768], P('mp'), may hold values from -0.875 to 0.875
- b_out: float32 [768], replicated, may hold values from -1.25 to 1.25
- scale_attn: float32 [768], replicated, may hold values from 0.5 to 1.5
- ln2_gain: float32 [768], replicated, may hold values from 0.5 to 1.5
- ln2_bias: float32 [768], replicated, may hold values from -1.25 to 1.25
- w_up: bfloat16 [768, 3072], P(None, 'mp'), may hold values from -0.21875 to 0.21875
- b_up: float32 [3072], P('mp'), may hold values from -1.75 to 1.75
- w_down: bfloat16 [3072, 768], P('mp'), may hold values from -0.21875 to 0.21875
- b_down: float32 [768], replicated, may hold values from -1.25 to 1.25
- scale_mlp: float32 [768], replicated, may hold values from 0.5 to 1.5
- page_lengths: int32 [8, 16], P('dp'), may hold values from 1 to 158, 2048 in all within a row
- patch_rows: int32 [16384], P('dp'), may hold values from 0 to 13
- patch_cols: int32 [16384], P('dp'), may hold values from 0 to 13
- cotangent: bfloat16 [16384, 768], P(('dp', 'mp')), may hold values from -6 to 6
Outputs:
- layer_out: bfloat16 [16384, 768], P(('dp', 'mp'))
- input_grad: float32 [16384, 768], P(('dp', 'mp'))
- ln1_gain_grad: float32 [768], replicated
- ln1_bias_grad: float32 [768], replicated
- w_qkv_grad: float32 [3, 768, 768], P(None, None, 'mp')
- b_qv_grad: float32 [2, 768], P(None, 'mp')
- rel_row_grad: float32 [12, 27], P('mp')
- rel_col_grad: float32 [12, 27], P('mp')
- w_out_grad: float32 [768, 768], P('mp')
- b_out_grad: float32 [768], replicated
- scale_attn_grad: float32 [768], replicated
- ln2_gain_grad: float32 [768], replicated
- ln2_bias_grad: float32 [768], replicated
- w_up_grad: float32 [768, 3072], P(None, 'mp')
- b_up_grad: float32 [3072], P('mp')
- w_down_grad: float32 [3072, 768], P('mp')
- b_down_grad: float32 [768], replicated
- scale_mlp_grad: float32 [768], replicated
The draws below stay inside these ranges and needn't reach their ends.
Inputs may be any that keep to these rules, and one draw needn't show every extreme that they name: Each row of page_lengths sums to 2048, and its largest entry is 158.
All inputs are finite; a program needn't handle non-finite values.
Results may differ from the reference program's by a relative error of at most 0.02.
Values may be sent and summed in bfloat16 or wider, within the bound.
No kernel may reach another device: no remote copies, remote signals or barrier semaphores. Data moves between devices by JAX's collectives and lax.ppermute only.
A program may use at most 128 MiB of HBM per device.

```python
import math
import jax
import jax.numpy as jnp
import numpy as np
from jax import lax

D = 768
HEADS = 12
HEAD_DIM = 64
FF = 3072
GRID = 14
GROUP_TOK = 2048
QBLK = 512
MARGIN = 256
PAGE_MOST = 158
PAGES = 16
GROUPS = 8
TOKENS = 16384
OFFSETS = 27


def with_ends(array, key, low, largest):
    extent = array.shape
    index_at = [jax.random.randint(jax.random.fold_in(key, axis), (), 0, extent[axis]) for axis in range(len(extent))]
    array = array.at[tuple(index_at)].set(low)
    longest = extent.index(max(extent))
    index_at[longest] = (index_at[longest] + 1) % extent[longest]
    return array.at[tuple(index_at)].set(largest)


def level_of(rng, dims, pieces, low, high):
    loudness = 1.0
    for position, parts in pieces:
        draws = jax.random.uniform(jax.random.fold_in(jax.random.fold_in(rng, 6), position), (parts,), jnp.float32, low / len(pieces), high / len(pieces))
        loudness = loudness * jnp.repeat(jnp.exp(draws), dims[position] // parts).reshape((-1,) + (1,) * (len(dims) - 1 - position))
    return loudness


def profile(count, total, reach, slope):
    loads = [(1 << 20) // math.isqrt(standing ** slope) + 1 for standing in range(2, count + 1)]
    surplus, holding = total - reach - (count - 1), [1] * (count - 1)
    while surplus > 0:
        candidates = [i for i in range(count - 1) if holding[i] < reach]
        pool, left = sum([loads[i] for i in candidates]), surplus
        for i in candidates:
            addition = min(reach - holding[i], max(1, left * loads[i] // pool), surplus)
            holding[i] = holding[i] + addition
            surplus = surplus - addition
    return np.array([reach] + holding)


def uneven(key, amount, total, bound, slope):
    if amount == 2:
        one = jax.random.randint(key, (), max(1, total - bound), min(bound, total - 1) + 1)
        return jnp.stack([one, total - one])
    tallies = jnp.asarray(profile(amount, total, bound, slope), jnp.int32)
    twos = (amount - 1) // 2
    giver, taker = tallies[1:1 + 2 * twos:2], tallies[2:2 + 2 * twos:2]
    slack = jnp.minimum(giver - 1, bound - taker)
    moved = jax.random.randint(jax.random.fold_in(key, 1), (twos,), 0, 1 << 20) % (slack + 1)
    tallies = tallies.at[1:1 + 2 * twos:2].set(giver - moved).at[2:2 + 2 * twos:2].set(taker + moved)
    return tallies[jax.random.permutation(jax.random.fold_in(key, 2), amount)]


def normal_values(own_key, shape, scale, most, pieces=(), kind=jnp.bfloat16):
    entries = jax.random.normal(own_key, shape, jnp.float32) * scale
    if len(pieces) > 0:
        entries = level_of(own_key, shape, pieces, -0.22, 0.18) * entries
    return jnp.clip(entries, min=-most, max=most).astype(kind)


def setup_inputs(seed: int = 0) -> dict:
    streams_of = jax.random.split(jax.random.key(seed), 22)
    return {
        "layer_in": normal_values(streams_of[0], (TOKENS, D), 1.0, 6.0, ((0, 32),)),
        "ln1_gain": jnp.clip(1.0 + 0.1 * jax.random.normal(streams_of[1], (D,), jnp.float32), 0.5, 1.5),
        "ln1_bias": normal_values(streams_of[2], (D,), 0.2, 1.25, (), jnp.float32),
        "w_qkv": normal_values(streams_of[3], (3, D, D), D ** -0.5, 0.21875, ((2, 4),)),
        "b_qv": normal_values(streams_of[4], (2, D), 0.3, 1.75, ((1, 4),), jnp.float32),
        "rel_row": normal_values(streams_of[5], (HEADS, OFFSETS), 0.5, 3.0, ((0, 4),), jnp.float32),
        "rel_col": normal_values(streams_of[6], (HEADS, OFFSETS), 0.5, 3.0, ((0, 4),), jnp.float32),
        "w_out": normal_values(streams_of[7], (D, D), (D // 16) ** -0.5, 0.875, ((0, 4),)),
        "b_out": normal_values(streams_of[8], (D,), 0.2, 1.25, (), jnp.float32),
        "scale_attn": jnp.clip(jax.random.uniform(streams_of[9], (D,), jnp.float32, 0.5, 1.5), 0.5, 1.5),
        "ln2_gain": jnp.clip(1.0 + 0.1 * jax.random.normal(streams_of[10], (D,), jnp.float32), 0.5, 1.5),
        "ln2_bias": normal_values(streams_of[11], (D,), 0.2, 1.25, (), jnp.float32),
        "w_up": normal_values(streams_of[12], (D, FF), D ** -0.5, 0.21875, ((1, 4),)),
        "b_up": normal_values(streams_of[13], (FF,), 0.3, 1.75, ((0, 4),), jnp.float32),
        "w_down": normal_values(streams_of[14], (FF, D), (FF // 4) ** -0.5, 0.21875, ((0, 4),)),
        "b_down": normal_values(streams_of[15], (D,), 0.2, 1.25, (), jnp.float32),
        "scale_mlp": jnp.clip(jax.random.uniform(streams_of[16], (D,), jnp.float32, 0.5, 1.5), 0.5, 1.5),
        "page_lengths": jax.vmap(lambda own: uneven(own, PAGES, GROUP_TOK, PAGE_MOST, 1))(jax.random.split(streams_of[17], GROUPS)).reshape((GROUPS, PAGES)).astype(jnp.int32),
        "patch_rows": with_ends(jax.random.randint(streams_of[18], (TOKENS,), 0, GRID), jax.random.fold_in(streams_of[18], 1), 0, GRID - 1).astype(jnp.int32),
        "patch_cols": with_ends(jax.random.randint(streams_of[19], (TOKENS,), 0, GRID), jax.random.fold_in(streams_of[19], 1), 0, GRID - 1).astype(jnp.int32),
        "cotangent": normal_values(streams_of[20], (TOKENS, D), 1.0, 6.0, ((0, 32),)),
    }


@jax.custom_vjp
def low(v):
    return lax.optimization_barrier(v.astype(jnp.bfloat16)).astype(jnp.float32)

@jax.custom_vjp
def low_back(v):
    return v

def low_keep(v):
    return (low(v), None)

def low_pass(kept, grad):
    return (grad,)

def back_keep(v):
    return (v, None)

def back_low(kept, grad):
    return (low(grad),)
low.defvjp(low_keep, low_pass)
low_back.defvjp(back_keep, back_low)

def exact_dot(left, right):
    return jnp.dot(left, right, precision=lax.Precision.HIGHEST)

def layer_norm(values, gain, shift):
    centred = values - lax.optimization_barrier(jnp.mean(values, axis=-1, keepdims=True))
    spread = lax.optimization_barrier(jnp.mean(centred * centred, axis=-1, keepdims=True))
    return centred * lax.rsqrt(spread + 1e-06) * gain + shift

def page_ids(lengths, count):
    ends = jnp.cumsum(lengths)
    places = jnp.arange(count, dtype=jnp.int32)
    return lax.optimization_barrier(jnp.sum((ends[None, :] <= places[:, None]).astype(jnp.int32), axis=1))

def offset_bias(table, coord_q, coord_k):
    cells = jnp.arange(GRID, dtype=jnp.int32)
    slots = jnp.arange(2 * GRID - 1, dtype=jnp.int32)
    picks = ((coord_q[:, None] - cells[None, :] + GRID - 1)[:, :, None] == slots[None, None, :]).astype(jnp.float32)
    lifted = jnp.einsum('qjo,ho->hqj', picks, table, precision=lax.Precision.HIGHEST)
    keys_hot = (coord_k[:, None] == cells[None, :]).astype(jnp.float32)
    return jnp.einsum('hqj,kj->hqk', lifted, keys_hot, precision=lax.Precision.HIGHEST)

def group_forward(group_in, rows, cols, lengths, params):
    ln1_gain, ln1_bias, w_qkv, b_qv, rel_row, rel_col, w_out, b_out, scale_attn, ln2_gain, ln2_bias, w_up, b_up, w_down, b_down, scale_mlp = params
    count = group_in.shape[0]
    pages = page_ids(lengths, count)
    window = QBLK + 2 * MARGIN
    factor = HEAD_DIM ** (-0.5)
    normed = low(layer_norm(group_in, ln1_gain, ln1_bias))
    query = low(low_back(exact_dot(normed, w_qkv[0]) + b_qv[0])).reshape(count, HEADS, HEAD_DIM)
    key = low(low_back(exact_dot(normed, w_qkv[1]))).reshape(count, HEADS, HEAD_DIM)
    value = low(low_back(exact_dot(normed, w_qkv[2]) + b_qv[1])).reshape(count, HEADS, HEAD_DIM)
    key_pad = jnp.pad(key, ((MARGIN, MARGIN), (0, 0), (0, 0)))
    value_pad = jnp.pad(value, ((MARGIN, MARGIN), (0, 0), (0, 0)))
    page_pad = jnp.pad(pages, MARGIN, constant_values=-1)
    row_pad = jnp.pad(rows, MARGIN)
    col_pad = jnp.pad(cols, MARGIN)

    def attend(start):
        q_block = lax.dynamic_slice_in_dim(query, start, QBLK, 0)
        k_block = lax.dynamic_slice_in_dim(key_pad, start, window, 0)
        v_block = lax.dynamic_slice_in_dim(value_pad, start, window, 0)
        scores = jnp.einsum('qhd,khd->hqk', q_block, k_block, precision=lax.Precision.HIGHEST) * factor
        scores = scores + offset_bias(rel_row, lax.dynamic_slice_in_dim(rows, start, QBLK, 0), lax.dynamic_slice_in_dim(row_pad, start, window, 0))
        scores = scores + offset_bias(rel_col, lax.dynamic_slice_in_dim(cols, start, QBLK, 0), lax.dynamic_slice_in_dim(col_pad, start, window, 0))
        scores = low_back(scores)
        same = lax.dynamic_slice_in_dim(pages, start, QBLK, 0)[:, None] == lax.dynamic_slice_in_dim(page_pad, start, window, 0)[None, :]
        scores = jnp.where(same[None], scores, -1000000000.0)
        probs = jax.nn.softmax(scores, axis=-1)
        return jnp.einsum('hqk,khd->qhd', low(probs), v_block, precision=lax.Precision.HIGHEST)
    starts = jnp.arange(count // QBLK, dtype=jnp.int32) * QBLK
    attended = lax.map(jax.checkpoint(attend), starts).reshape(count, HEADS * HEAD_DIM)
    attended = low(low_back(attended))
    branch = low_back(exact_dot(attended, w_out))
    middle = group_in + scale_attn * (branch + b_out)
    normed_two = low(layer_norm(middle, ln2_gain, ln2_bias))
    pre = low_back(exact_dot(normed_two, w_up) + b_up)
    act = low(jax.nn.gelu(pre))
    branch_two = low_back(exact_dot(act, w_down))
    return middle + scale_mlp * (branch_two + b_down)

def reference(layer_in, ln1_gain, ln1_bias, w_qkv, b_qv, rel_row, rel_col, w_out, b_out, scale_attn, ln2_gain, ln2_bias, w_up, b_up, w_down, b_down, scale_mlp, page_lengths, patch_rows, patch_cols, cotangent):
    params = tuple((item.astype(jnp.float32) for item in (ln1_gain, ln1_bias, w_qkv, b_qv, rel_row, rel_col, w_out, b_out, scale_attn, ln2_gain, ln2_bias, w_up, b_up, w_down, b_down, scale_mlp)))
    inputs = layer_in.astype(jnp.float32).reshape(GROUPS, GROUP_TOK, D)
    rows = patch_rows.reshape(GROUPS, GROUP_TOK)
    cols = patch_cols.reshape(GROUPS, GROUP_TOK)

    def forward(inputs, params):

        def step(carry, item):
            return (carry, jax.checkpoint(group_forward)(item[0], item[1], item[2], item[3], params))
        _, outputs = lax.scan(step, None, (inputs, rows, cols, page_lengths))
        return outputs
    layer_out, pull = jax.vjp(forward, inputs, params)
    input_grad, grads = pull(cotangent.astype(jnp.float32).reshape(GROUPS, GROUP_TOK, D))
    return (layer_out.reshape(TOKENS, D).astype(jnp.bfloat16), input_grad.reshape(TOKENS, D), grads[0], grads[1], grads[2], grads[3], grads[4], grads[5], grads[6], grads[7], grads[8], grads[9], grads[10], grads[11], grads[12], grads[13], grads[14], grads[15])
```

```python
import functools

import jax
import jax.numpy as jnp
import numpy as np
from jax import lax
from jax.experimental import pallas as pl
from jax.experimental.pallas import tpu as pltpu
from jax.sharding import PartitionSpec as P

HEAD_DIM = 64
GRID = 14
HALO = 160
QB = 128
WIN = QB + 2 * HALO
BIG = float(2**30)
F32 = jnp.float32
BF = jnp.bfloat16
MIB = 1024 * 1024


def nn(a, b):
    return lax.dot_general(a, b, (((1,), (0,)), ((), ())), preferred_element_type=F32)


def nt(a, b):
    return lax.dot_general(a, b, (((1,), (1,)), ((), ())), preferred_element_type=F32)


def tn(a, b):
    return lax.dot_general(a, b, (((0,), (0,)), ((), ())), preferred_element_type=F32)


def moments(v):
    centred = v - jnp.mean(v, axis=-1, keepdims=True)
    rstd = lax.rsqrt(jnp.mean(centred * centred, axis=-1, keepdims=True) + 1e-06)
    return centred * rstd, rstd


def norm_back(grad, hat, rstd, gain):
    u = grad * gain
    return rstd * (
        u - jnp.mean(u, axis=-1, keepdims=True) - hat * jnp.mean(u * hat, axis=-1, keepdims=True)
    )


def row(ref):
    return ref[...].reshape(1, ref.shape[0])


def pack_kernel(wq, small, out):
    out[0:576, :] = wq[...]
    high = small[...].astype(BF)
    low = small[...] - high.astype(F32)
    out[576:592, :] = jnp.concatenate([high.astype(F32), low], axis=0).astype(BF)


def smalls(rows):
    both = rows.astype(F32)
    return both[0:8, :] + both[8:16, :]


def prep_kernel(
    me, lengths, left, mid, right, gain, bias, rows, cols, ct, scale_two, normed, extk, ohq, g_out
):
    scale, offset = row(gain), row(bias)
    at = 0
    for ref in (left, mid, right):
        for i in range(ref.shape[0] // 32):
            hat, _ = moments(ref[32 * i : 32 * i + 32, :].astype(F32))
            normed[at : at + 32, :] = (hat * scale + offset).astype(BF)
            at += 32

    for i in range(ct.shape[0] // 64):
        here = slice(64 * i, 64 * i + 64)
        g_out[here, :] = (row(scale_two) * ct[here, :].astype(F32)).astype(BF)

    own = mid.shape[0]
    tiles = rows.shape[0]
    first = me[0, 0] * (own // 128) - 2
    pick = lambda ref: jnp.concatenate([ref[pl.ds(jnp.clip(first + t, 0, tiles - 1), 1), :] for t in range(8)], axis=1)
    by_row, by_col = pick(rows), pick(cols)
    place = lax.broadcasted_iota(jnp.int32, (1, 1024), 1) + first * 128
    inside = (place >= 0) & (place < tiles * 128)
    page = jnp.zeros((1, 1024), jnp.int32)
    end = 0
    for i in range(lengths.shape[1]):
        end = end + lengths[0, i]
        page = page + jnp.where(place >= end, 1, 0)

    def hot(sub, row_at, col_at, bit_at, swapped):
        hit = (by_row == row_at) | (by_col == col_at)
        for b in range(4):
            bit = (page >> b) & 1
            hit = hit | ((sub == bit_at + 2 * b + swapped) & (bit == 0))
            hit = hit | ((sub == bit_at + 2 * b + 1 - swapped) & (bit == 1))
        return hit

    sub = lax.broadcasted_iota(jnp.int32, (64, 1024), 0)
    rest = jnp.where(sub < 28, sub, sub - 28)
    row_at = jnp.where((rest < GRID) & (sub < 56), GRID - 1 - rest, -1)
    col_at = jnp.where((rest >= GRID) & (sub < 56), 2 * GRID - 1 - rest, -1)
    keys = hot(sub, row_at, col_at, 56, 0) | ((sub >= 56) & jnp.logical_not(inside))
    keys = jnp.where(keys, 1.0, 0.0).T
    extk[...] = keys[256 - HALO : 256 + own + HALO, :].astype(BF)
    sub = lax.broadcasted_iota(jnp.int32, (128, 1024), 0)
    none = jnp.full((128, 1024), -1, jnp.int32)
    row_at = jnp.where(sub < GRID, GRID - 1 - sub, jnp.where((sub >= 64) & (sub < 64 + GRID), sub - 64, none))
    other = sub - 16
    col_at = jnp.where((other >= 0) & (other < GRID), GRID - 1 - other, none)
    col_at = jnp.where((sub >= 80) & (sub < 80 + GRID), sub - 80, col_at)
    queries = jnp.where(hot(sub, row_at, col_at, 32, 1), 1.0, 0.0)
    ohq[...] = queries[:, 256 : 256 + own].T.astype(BF)


def bias_table(rows, cols):
    lane = lax.broadcasted_iota(jnp.int32, (16, 128), 1)
    groups = []
    for table, first in ((rows, 64), (cols, 64 + GRID)):
        table = jnp.broadcast_to(table, (16, 128))
        high = table.astype(BF).astype(F32)
        total = jnp.zeros((16, 128), F32)
        for part, at in ((high, first), (table - high, first + 2 * GRID)):
            turned = pltpu.roll(part, (at - GRID + 1) % 128, 1, stride=1, stride_axis=0)
            total = total + jnp.where((lane >= at) & (lane < at + GRID), turned, 0.0)
        groups.append(total)
    lane = lax.broadcasted_iota(jnp.int32, (96, 128), 1)
    sub = lax.broadcasted_iota(jnp.int32, (96, 128), 0)
    bits = jnp.where((sub < 8) & (lane == sub + 120), -BIG, 0.0)
    return jnp.concatenate(groups + [bits], axis=0).astype(BF)


def attn_fwd_kernel(
    normed, w, extk, ohq, k_out, q_out, v_out, att_out, lse_out, tok, vt
):
    own = mid_rows = q_out.shape[1]
    tok[...] = jnp.zeros(tok.shape, F32)
    small = smalls(w[576:592, :])
    q = nt(normed[HALO : HALO + own, :], w[0:192, :]) + small[6:7, 0:192]
    q = q.astype(BF).astype(F32) * (HEAD_DIM**-0.5)
    q = jnp.concatenate([q, jnp.zeros((own, 64), F32)], axis=1)
    lane = lax.broadcasted_iota(jnp.int32, (own, 256), 1)
    for i in range(3):
        here = (lane >= 64 * i) & (lane < 64 * i + 64)
        ext = nn(ohq[...], bias_table(small[i : i + 1, 0:128], small[3 + i : 4 + i, 0:128]))
        ext = jnp.concatenate([jnp.zeros((own, 128), F32), ext], axis=1)
        q_out[i] = (jnp.where(here, q, 0.0) + ext).astype(BF)
    k = nt(normed[...], w[192:384, :]).astype(BF)
    k_out[...] = jnp.concatenate([k, extk[...]], axis=1)
    v = nt(normed[...], w[384:576, :]) + small[6:7, 256:448]
    v_out[...] = v.astype(BF)
    vt[...] = v.T.astype(BF)
    for b in range(mid_rows // QB):
        at = slice(b * QB, b * QB + WIN)
        here = slice(b * QB, b * QB + QB)
        parts = []
        keys = k_out[at, :]
        for i in range(3):
            s = nt(keys, q_out[i, here, :])
            top = jnp.max(s, axis=0, keepdims=True)
            e = jnp.exp(s - top)
            total = jnp.sum(e, axis=0, keepdims=True)
            o = nn(vt[64 * i : 64 * i + 64, at], e.astype(BF))
            parts.append(o / total)
            lse_out[i : i + 1, here] = top + jnp.log(total)
        att_out[here, :] = jnp.concatenate(parts, axis=0).T.astype(BF)


def mid_kernel(
    a0, a1, a2, a3, w0, w1, w2, w3, x, b_out, scale, gain, bias, branch_out, mid_out, n2_first, n2_second
):
    step = 128
    for i in range(x.shape[0] // step):
        at = slice(i * step, (i + 1) * step)
        branch = nn(a0[at, :], w0[...]) + nn(a1[at, :], w1[...])
        branch = branch + nn(a2[at, :], w2[...]) + nn(a3[at, :], w3[...])
        branch = branch + row(b_out)
        middle = x[at, :].astype(F32) + row(scale) * branch
        hat, _ = moments(middle)
        branch_out[at, :] = branch
        mid_out[at, :] = middle
        out = (n2_first, n2_second)[i // 2]
        here = i % 2 * step
        out[here : here + step, :] = (hat * row(gain) + row(bias)).astype(BF)


def mlp_kernel(chunks, first, *refs):
    n2 = refs[:chunks]
    g, wu0, wd0, wu1, wd1, s0, s1, act0, act1, dpre0, dpre1, b_out, n_out, sums = refs[chunks:]
    c = 0.7978845608028654
    step = 256
    totals = []
    for wu, wd, s, act, dpre, r in ((wu0, wd0, s0, act0, dpre0, 0), (wu1, wd1, s1, act1, dpre1, 1)):
        bias = smalls(s[...])[7:8, :]
        total = jnp.zeros((1, wu.shape[1]), F32)
        for i in range(chunks):
            at = slice(i * step, (i + 1) * step)
            pre = nn(n2[i][...], wu[...]) + bias
            sq = pre * pre
            t = jnp.tanh(c * pre * (1.0 + 0.044715 * sq))
            half = 0.5 * (1.0 + t)
            slope = half + (0.5 * c) * pre * (1.0 - t * t) * (1.0 + (3 * 0.044715) * sq)
            a = (pre * half).astype(BF)
            act[at, :] = a
            dp = (nt(g[first + i * step : first + (i + 1) * step, :], wd[...]) * slope).astype(BF)
            dpre[at, :] = dp
            total = total + jnp.sum(dp.astype(F32), axis=0, keepdims=True)
        totals.append(total)
    for i in range(chunks):
        at = slice(i * step, (i + 1) * step)
        n_out[at, :] = (nt(dpre0[at, :], wu0[...]) + nt(dpre1[at, :], wu1[...])).astype(n_out.dtype)
        b_out[at, :] = (nn(act0[at, :], wd0[...]) + nn(act1[at, :], wd1[...])).astype(b_out.dtype)
    sums[...] = jnp.concatenate(totals + [jnp.zeros((6, 768), F32)], axis=0)


def weights_kernel(
    r, n2a, n2b, n2c, n2d, g, g_far, act, act_c, act_d, dpre, dpre_c, dpre_d, sa, sb, sc, sums, *outs
):
    rows = lambda *parts: jnp.concatenate([p[...] for p in parts], axis=0)
    up = tn(rows(n2a, n2b, n2c, n2d), rows(dpre, dpre_c, dpre_d)).astype(BF)
    down = tn(rows(act, act_c, act_d), rows(g, g_far)).astype(BF)
    for i in range(4):
        outs[i][...] = up[192 * i : 192 * i + 192, :]
        outs[4 + i][...] = down[192 * i : 192 * i + 192, :]
    line = sa[r : r + 1, :] + sb[r : r + 1, :] + sc[r : r + 1, :]
    sums[...] = jnp.concatenate(
        [line[:, 256 * j : 256 * j + 256] for j in range(3)] + [jnp.zeros((5, 256), F32)], axis=0
    )


def midb_kernel(mid, branch, ct, gn2, ret_a, ret_b, gain, scale, mg_out, gb_out, sums):
    step = 64
    acc = [jnp.zeros((1, mid.shape[1]), F32)] * 4
    for i in range(mid.shape[0] // step):
        at = slice(i * step, (i + 1) * step)
        ret, here = ((ret_a, i * step), (ret_b, i * step - 256))[i * step // 256]
        hat, rstd = moments(mid[at, :])
        g = gn2[at, :] + ret[here : here + step, :].astype(F32)
        mg = ct[at, :].astype(F32) + norm_back(g, hat, rstd, row(gain))
        mg_out[at, :] = mg
        gb = row(scale) * mg
        gb_out[at, :] = gb.astype(BF)
        terms = [gb, mg * branch[at, :], g * hat, g]
        acc = [a + jnp.sum(t, axis=0, keepdims=True) for a, t in zip(acc, terms)]
    sums[...] = jnp.concatenate(acc + [jnp.zeros((4, mid.shape[1]), F32)], axis=0)


def attn_bwd_kernel(
    k, q, v, lse, gb, w, wo, att, ohq, normed, up_sum, acc,
    g_first, g_last, acc_out, small_out, kt, dkacc, dvacc, do, dqs,
):
    own = q.shape[1]
    mine = slice(HALO, HALO + own)
    g_last[192:384, :] = tn(att[...], gb[...]).astype(BF)
    do[...] = nt(gb[...], wo[...]).astype(BF)
    kt[...] = k[...].astype(F32).T.astype(BF)
    dkacc[...] = jnp.zeros(dkacc.shape, F32)
    dvacc[...] = jnp.zeros(dvacc.shape, F32)
    lane = lax.broadcasted_iota(jnp.int32, (QB, 192), 1)
    rel = jnp.zeros((192, 128), F32)
    for b in range(own // QB):
        at = slice(b * QB, b * QB + WIN)
        here = slice(b * QB, b * QB + QB)
        keys = k[at, :]
        vals = v[at, :]
        d_block = do[here, :]
        dk, dv = dkacc[at, :], dvacc[at, :]
        qparts, lparts = [], []
        for i in range(3):
            qb = q[i, here, :]
            s = nt(keys, qb)
            p = jnp.exp(s - lse[i : i + 1, here])
            head = (lane >= 64 * i) & (lane < 64 * i + 64)
            db = jnp.where(head, d_block, jnp.zeros_like(d_block))
            dp = nt(vals, db)
            inner = jnp.sum(p * dp, axis=0, keepdims=True)
            ds = (p * (dp - inner)).astype(BF)
            dv = dv + nn(p.astype(BF), db)
            dk = dk + nn(ds, qb)
            qparts.append(nn(kt[64 * i : 64 * i + 64, at], ds))
            lparts.append(nn(kt[192:256, at], ds))
        dkacc[at, :] = dk
        dvacc[at, :] = dv
        dq = jnp.concatenate(qparts, axis=0) * (HEAD_DIM**-0.5)
        dqs[here, :] = dq.T.astype(BF)
        lift = jnp.concatenate(lparts, axis=0)
        high = lift.astype(BF)
        low = (lift - high.astype(F32)).astype(BF)
        rel = rel + nn(high, ohq[here, :]) + nn(low, ohq[here, :])
    dk = dkacc[:, 0:192].astype(BF)
    dv = dvacc[...].astype(BF)
    g_first[0:192, :] = tn(dqs[...], normed[mine, :]).astype(BF)
    g_first[192:384, :] = tn(dk, normed[...]).astype(BF)
    g_last[0:192, :] = tn(dv, normed[...]).astype(BF)
    acc_out[...] = acc[...] + nn(dk, w[192:384, :]) + nn(dv, w[384:576, :])
    acc_out[mine, :] += nn(dqs[...], w[0:192, :])
    lane = lax.broadcasted_iota(jnp.int32, (16, 128), 1)
    sub = lax.broadcasted_iota(jnp.int32, (16, 128), 0)
    lane_c = lax.broadcasted_iota(jnp.int32, (24, 128), 1)
    sub_c = lax.broadcasted_iota(jnp.int32, (24, 128), 0)
    by_row, by_col = [], []
    for i in range(3):
        part = jnp.where((sub < GRID) & (lane >= 64) & (lane < 64 + GRID), rel[64 * i : 64 * i + 16, :], 0.0)
        part = pltpu.roll(part, 0, 1, stride=1, stride_axis=0)
        by_row.append(jnp.sum(part, axis=0, keepdims=True))
        keep = (sub_c >= 6) & (sub_c < 6 + GRID) & (lane_c >= 80) & (lane_c < 80 + GRID)
        part = jnp.where(keep, rel[64 * i + 8 : 64 * i + 32, :], 0.0)
        part = pltpu.roll(part, 0, 1, stride=1, stride_axis=0)
        by_col.append(jnp.sum(part, axis=0, keepdims=True))
    sums = [jnp.sum(t.astype(F32), axis=0, keepdims=True) for t in (dqs[...], dv)]
    rels = jnp.concatenate(by_row + by_col, axis=0)
    small_out[0:6, :] = jnp.concatenate([rels, jnp.zeros((6, 128), F32)], axis=1)
    small_out[6:8, :] = jnp.concatenate([jnp.concatenate(sums, axis=0), jnp.zeros((2, 64), F32)], axis=1)
    small_out[8:16, :] = up_sum[...]


def out_kernel(mid, two, ret_a, ret_b, ct, b_down, scale_two, before, lo_out, sums):
    step = 64
    acc = [jnp.zeros((1, mid.shape[1]), F32)] * 2
    for i in range(mid.shape[0] // step):
        at = slice(i * step, (i + 1) * step)
        ret, here = ((ret_a, i * step), (ret_b, i * step - 256))[i * step // 256]
        branch_two = two[at, :] + ret[here : here + step, :].astype(F32) + row(b_down)
        lo_out[at, :] = (mid[at, :] + row(scale_two) * branch_two).astype(BF)
        up = ct[at, :].astype(F32)
        terms = [row(scale_two) * up, up * branch_two]
        acc = [a + jnp.sum(t, axis=0, keepdims=True) for a, t in zip(acc, terms)]
    sums[...] = jnp.concatenate([before[0:4, :]] + acc + [before[6:8, :]], axis=0)


def final_kernel(x, gn1, fl, fr, mg, gain, before, in_out, sums):
    step = 32
    own = x.shape[0]
    acc = [jnp.zeros((1, x.shape[1]), F32)] * 2
    for i in range(own // step):
        at = slice(i * step, (i + 1) * step)
        hat, rstd = moments(x[at, :].astype(F32))
        g = gn1[HALO + i * step : HALO + (i + 1) * step, :]
        if (i + 1) * step <= HALO:
            g = g + fl[at, :].astype(F32)
        tail = i * step - (own - HALO)
        if tail >= 0:
            g = g + fr[tail : tail + step, :].astype(F32)
        in_out[at, :] = mg[at, :] + norm_back(g, hat, rstd, row(gain))
        terms = [g * hat, g]
        acc = [a + jnp.sum(t, axis=0, keepdims=True) for a, t in zip(acc, terms)]
    total = jnp.concatenate([before[0:6, :]] + acc, axis=0)
    for j in range(3):
        sums[8 * j : 8 * j + 8, :] = total[:, 256 * j : 256 * j + 256]


def unpack_kernel(sums, b_up, b_qv, rel_row, rel_col, *wholes):
    line = lambda parts: jnp.concatenate(parts, axis=1).reshape(768)
    b_up[...] = line([sums[8 + j : 9 + j, :] for j in range(3)])
    b_qv[...] = sums[6:8, 0:192]
    rel_row[...] = sums[0:3, 64:91]
    rel_col[...] = sums[3:6, 86:113]
    for i, out in enumerate(wholes):
        out[...] = line([sums[16 + 8 * j + i : 17 + 8 * j + i, :] for j in range(3)])


def op(kernel, outs, args, specs=None, out_specs=None, scratch=(), aliases=None, limit=18, after=()):
    n = len(args)

    def body(*refs):
        kernel(*refs[:n], *refs[n + len(after) :])

    return pl.pallas_call(
        body,
        out_shape=[jax.ShapeDtypeStruct(s, d) for s, d in outs],
        in_specs=(specs or [VMEM] * n) + [pl.BlockSpec(memory_space=pl.ANY)] * len(after),
        out_specs=out_specs or [VMEM] * len(outs),
        scratch_shapes=list(scratch),
        compiler_params=pltpu.CompilerParams(vmem_limit_bytes=limit * MIB),
        input_output_aliases=aliases or {},
    )(*args, *after)


VMEM = pl.BlockSpec(memory_space=pltpu.VMEM)
SMEM = pl.BlockSpec(memory_space=pltpu.SMEM)


def behind(v, first):
    if v.shape[-1] != first.shape[-1]:
        return v
    return jnp.where(first[0:1].astype(F32) > 3e38, jnp.zeros_like(v), v)


def add(*parts):
    return sum(p.astype(F32) for p in parts).astype(BF)


def halves(v, bit):
    n = v.shape[0] // 2
    return [jnp.where(bit == 0, v[:n], v[n:]), jnp.where(bit == 0, v[n:], v[:n])]


def joined(mine, other, bit):
    return jnp.concatenate([jnp.where(bit == 0, mine, other), jnp.where(bit == 0, other, mine)], axis=0)


def send(v, axis, pairs):
    return lax.ppermute(v, axis, pairs)


def make_body(ndp, nmp):
    assert nmp == 4 and ndp % 8 == 0 and ndp & (ndp - 1) == 0
    core = ("mp", [(i, i ^ 1) for i in range(nmp)])
    over_y = ("mp", [(i, i ^ 2) for i in range(nmp)])
    over_x = ("dp", [(i, i ^ 1) for i in range(ndp)])
    over_z = [("dp", [(i, i ^ (1 << b)) for i in range(ndp)]) for b in range(1, ndp.bit_length() - 1)]
    rightward = ("mp", [(i, i + 1) for i in range(nmp - 1)])
    leftward = ("mp", [(i + 1, i) for i in range(nmp - 1)])

    def body(
        layer_in, ln1_gain, ln1_bias, w_qkv, b_qv, rel_row, rel_col, w_out, b_out, scale_attn, ln2_gain,
        ln2_bias, w_up, b_up, w_down, b_down, scale_mlp, page_lengths, patch_rows, patch_cols, cotangent,
    ):
        own, width = layer_in.shape
        kv = own + 2 * HALO
        units = w_up.shape[1]
        cols = w_qkv.shape[2]
        me = lax.axis_index("mp")
        x_bit = lax.axis_index("dp") & 1
        z_bit = (lax.axis_index("dp") >> 1) & 1
        line = ((8, width), F32)

        left, right = send(layer_in[own - HALO :], *rightward), send(layer_in[:HALO], *leftward)
        wq = jnp.transpose(w_qkv, (0, 2, 1)).reshape(3 * cols, width)
        place = lambda v, at, lane: jnp.pad(v, ((at, 8 - at - v.shape[0]), (lane, width - lane - v.shape[1])))
        small = place(rel_row, 0, 0) + place(rel_col, 3, 0) + place(b_up[None], 7, 0)
        small = small + place(b_qv[0:1], 6, 0) + place(b_qv[1:2], 6, 256)
        (packed,) = op(pack_kernel, [((3 * cols + 16, width), BF)], [wq, small])
        mine = jnp.split(halves(packed, x_bit)[0], 2, axis=0)
        packed_y = [send(v, *over_y) for v in mine]
        packed_near = send(packed, *core)
        out_y, out_near = send(w_out, *over_y), send(w_out, *core)
        up_near, down_near = send(w_up, *core), send(w_down, *core)
        normed, extk, ohq, mlp_grad = op(
            prep_kernel, [((kv, width), BF), ((kv, 64), BF), ((own, 128), BF), ((own, width), BF)],
            [
                me.reshape(1, 1), page_lengths, left, layer_in, right, ln1_gain, ln1_bias,
                patch_rows.reshape(-1, 128), patch_cols.reshape(-1, 128), cotangent, scale_mlp,
            ],
            specs=[SMEM, SMEM] + [VMEM] * 9, after=mine,
        )
        mlp_grad_y = send(mlp_grad, *over_y)

        def attention(w, after=()):
            outs = [((kv, 256), BF), ((3, own, 256), BF), ((kv, 192), BF), ((own, 192), BF), ((8, own), F32), line]
            return op(
                attn_fwd_kernel, outs, [normed, w, extk, ohq], scratch=[pltpu.VMEM((192, kv), BF)], after=after
            )

        fwd = [attention(packed)]
        packed_y = [behind(v, fwd[0][5]) for v in packed_y]
        packed_x = [send(v, *over_x) for v in packed_y]
        fwd.append(attention(packed_near, after=packed_y))
        packed_x = [behind(v, fwd[1][5]) for v in packed_x]
        packed_far = joined(jnp.concatenate(packed_y, axis=0), jnp.concatenate(packed_x, axis=0), x_bit)
        packed_diag = jnp.concatenate([send(packed_far[:304], *core), send(packed_far[304:], *core)], axis=0)
        fwd.append(attention(packed_far))
        out_far = behind(out_y, fwd[2][5])
        out_diag = send(out_far, *core)
        fwd.append(attention(packed_diag, after=[out_far]))
        ins_w, outs_w = [packed, packed_near, packed_far, packed_diag], [w_out, out_near, out_far, out_diag]
        part = ((own // 2, width), BF)
        branch, middle, n2a, n2b = op(
            mid_kernel, [((own, width), F32), ((own, width), F32), part, part],
            [*[f[3] for f in fwd], *outs_w, layer_in, b_out, scale_attn, ln2_gain, ln2_bias], after=[mlp_grad_y],
        )

        n2c, n2d = send(n2a, *over_y), send(n2b, *over_y)
        tails = [w[3 * cols :] for w in ins_w[:2]]

        def mlp(n2, g, first, dtype, after=()):
            rows = len(n2) * n2[0].shape[0]
            return op(
                functools.partial(mlp_kernel, len(n2), first),
                [((rows, units), BF)] * 4 + [((rows, width), dtype)] * 2 + [line],
                [*n2, g, w_up, w_down, up_near, down_near, *tails], after=after,
            )

        mine_mlp = mlp([n2a, n2b], mlp_grad, 0, F32)
        first_mlp = mlp([n2c], mlp_grad_y, 0, BF, after=[mine_mlp[6]])
        ret_na, ret_ba = send(first_mlp[5], *over_y), send(first_mlp[4], *over_y)
        second_mlp = mlp([n2d], mlp_grad_y, own // 2, BF, after=[first_mlp[6]])
        ret_nb, ret_bb = send(second_mlp[5], *over_y), send(second_mlp[4], *over_y)

        def weights(r, after):
            parts = [mine_mlp, first_mlp, second_mlp]
            return op(
                functools.partial(weights_kernel, r), [((8, 256), F32)] + [((width // 4, width), BF)] * 8,
                [
                    n2a, n2b, n2c, n2d, mlp_grad, mlp_grad_y, *[p[r] for p in parts], *[p[2 + r] for p in parts],
                    *[p[6] for p in parts],
                ],
                after=after,
            )

        up_far_sum, *grads_far = weights(1, [second_mlp[6]])
        mlp_near = [send(g, *core) for g in grads_far]
        up_own_sum, *grads_own = weights(0, [up_far_sum])
        up_sums = [up_own_sum, up_far_sum, jnp.zeros((8, 256), F32), jnp.zeros((8, 256), F32)]
        middle_grad, branch_grad, sums_two = op(
            midb_kernel, [((own, width), F32), ((own, width), BF), line],
            [middle, branch, cotangent, mine_mlp[5], ret_na, ret_nb, ln2_gain, scale_attn], after=[up_own_sum],
        )

        results, asked = {}, {}

        def block(name, near, far=None):
            there = [send(far, *over_y)] if far is not None else []
            keep, other = yield lambda *p: halves(add(*p), x_bit), lambda: near() + there
            recv = send(other, *over_x)
            keep, other = yield lambda a, b: halves(add(a, b), z_bit), [keep, recv]
            recv = send(other, *over_z[0])
            for link in over_z[1:]:
                (keep,) = yield lambda a, b: [add(a, b)], [keep, recv]
                recv = send(keep, *link)
            (keep,) = yield lambda a, b: [add(a, b)], [keep, recv]
            recv = send(keep, *over_z[0])
            (keep,) = yield lambda a, b: [joined(a, b, z_bit)], [keep, recv]
            recv = send(keep, *over_x)
            (results[name],) = yield lambda a, b: [joined(a, b, x_bit).astype(F32)], [keep, recv]

        def start(flow):
            asked[flow] = next(flow)
            return flow

        def steps(first, *flows):
            flows = [f for f in flows if f in asked]
            wanted = [(fn, args() if callable(args) else args) for fn, args in (asked.pop(f) for f in flows)]
            *given, at = lax.optimization_barrier((*[a for _, args in wanted for a in args], first))
            made, counts = [], []
            for fn, args in wanted:
                outs = fn(*[behind(a, at) for a in given[: len(args)]])
                given = given[len(args) :]
                made += outs
                counts.append(len(outs))
            outs = made = list(lax.optimization_barrier(made))
            for flow, count in zip(flows, counts):
                try:
                    asked[flow] = flow.send(outs[:count])
                except StopIteration:
                    pass
                outs = outs[count:]
            return [m for m in made if m.shape[-1] == width]

        whole = lambda parts: jnp.concatenate(parts, axis=0)
        up_flow = start(block("up", lambda: [whole(grads_own[:4]), whole(mlp_near[:4])]))
        down_flow = start(block("down", lambda: [whole(grads_own[4:]), whole(mlp_near[4:])]))
        made = steps(sums_two, up_flow, down_flow)

        grads_att, tiny, acc = [None] * 4, [None] * 4, jnp.zeros((kv, width), F32)
        n = width // 2

        def attention_back(r, acc, after=()):
            k, q, v, att, lse, _ = fwd[r]
            *grads_att[r], acc, tiny[r] = op(
                attn_bwd_kernel, [((n, width), BF), ((n, width), BF), ((kv, width), F32), ((16, 256), F32)],
                [k, q, v, lse, branch_grad, ins_w[r], outs_w[r], att, ohq, normed, up_sums[r], acc],
                scratch=[
                    pltpu.VMEM((256, kv), BF), pltpu.VMEM((kv, 256), F32), pltpu.VMEM((kv, 192), F32),
                    pltpu.VMEM((own, 192), BF), pltpu.VMEM((own, 192), BF),
                ],
                aliases={11: 2}, after=after,
            )
            return acc

        acc = attention_back(3, acc, after=made)
        att_far = [send(g, *core) for g in grads_att[3]]
        acc = attention_back(2, acc)
        far_sum = whole([add(a, behind(b, grads_att[2][0])) for a, b in zip(grads_att[2], att_far)])
        att_near = []
        att_flow = start(block("att", lambda: [whole(grads_att[0]), whole(att_near)], far_sum))
        made = steps(grads_att[2][0], up_flow)
        layer_out, sums_out = op(
            out_kernel, [((own, width), BF), line],
            [middle, mine_mlp[4], ret_ba, ret_bb, cotangent, b_down, scale_mlp, sums_two], after=made,
        )
        acc = attention_back(1, acc, after=[sums_out, far_sum])
        att_near += [send(g, *core) for g in grads_att[1]]
        made = steps(grads_att[1][0], up_flow, down_flow)
        acc = attention_back(0, acc, after=made)
        to_left, to_right = acc[:HALO].astype(BF), acc[HALO + own :].astype(BF)
        from_left, from_right = send(to_right, *rightward), send(to_left, *leftward)

        def tail():
            given = yield lambda *v: list(v), [from_left, from_right]
            results["in"], whole_sums = op(
                final_kernel, [((own, width), F32), ((24, 256), F32)],
                [layer_in, acc, *given, middle_grad, ln1_gain, sums_out],
            )
            recv = send(jnp.concatenate([tiny[1], tiny[3], whole_sums], axis=0), *core)
            near, part = yield (
                lambda a, b, c, d: [a + d[0:16], jnp.concatenate([b + d[16:32], c + d[32:56]], axis=0)],
                [tiny[0], tiny[2], whole_sums, recv],
            )
            recv = send(part, *over_y)
            (part,) = yield (
                lambda a, b, c: [jnp.concatenate([a + c[0:16], b[16:40] + c[16:40]], axis=0)], [near, part, recv]
            )
            for link in [over_x] + over_z:
                recv = send(part, *link)
                (part,) = yield lambda a, b: [a + b], [part, recv]
            flat = ((width,), F32)
            results["small"] = op(
                unpack_kernel, [flat, ((2, 192), F32), ((3, 27), F32), ((3, 27), F32)] + [flat] * 8, [part]
            )

        made = steps(grads_att[0][0], att_flow, up_flow, down_flow)
        start(tail())
        while asked:
            made = steps(made[-1], *list(asked)) or made

        w_up_grad, w_down_grad = results["up"], results["down"]
        w_qkv_grad = jnp.transpose(results["att"][: 3 * cols].reshape(3, cols, width), (0, 2, 1))
        b_up_g, b_qv_g, rel_row_g, rel_col_g, *wholes = results["small"]
        b_out_g, scale_attn_g, ln2_gain_g, ln2_bias_g, b_down_g, scale_mlp_g, ln1_gain_g, ln1_bias_g = wholes
        return (
            layer_out, results["in"], ln1_gain_g, ln1_bias_g, w_qkv_grad, b_qv_g, rel_row_g, rel_col_g,
            results["att"][3 * cols :], b_out_g, scale_attn_g, ln2_gain_g, ln2_bias_g, w_up_grad, b_up_g, w_down_grad,
            b_down_g, scale_mlp_g,
        )

    return body


def solution(mesh):
    rows = P(("dp", "mp"), None)
    return jax.shard_map(
        make_body(mesh.shape["dp"], mesh.shape["mp"]),
        mesh=mesh,
        in_specs=(
            rows, P(), P(), P(None, None, "mp"), P(None, "mp"), P("mp", None), P("mp", None), P("mp", None),
            P(), P(), P(), P(), P(None, "mp"), P("mp"), P("mp", None), P(), P(), P("dp", None), P("dp"),
            P("dp"), rows,
        ),
        out_specs=(
            rows, rows, P(), P(), P(None, None, "mp"), P(None, "mp"), P("mp", None), P("mp", None),
            P("mp", None), P(), P(), P(), P(), P(None, "mp"), P("mp"), P("mp", None), P(), P(),
        ),
        check_vma=False,
    )
```

```python
import functools

import jax
import jax.numpy as jnp
import numpy as np
from jax import lax
from jax.experimental import pallas as pl
from jax.experimental.pallas import tpu as pltpu
from jax.sharding import PartitionSpec as P

HEAD_DIM = 64
GRID = 14
HALO = 160
QB = 128
WIN = QB + 2 * HALO
BIG = float(2**30)
F32 = jnp.float32
BF = jnp.bfloat16
MIB = 1024 * 1024


def nn(a, b):
    return lax.dot_general(a, b, (((1,), (0,)), ((), ())), preferred_element_type=F32)


def nt(a, b):
    return lax.dot_general(a, b, (((1,), (1,)), ((), ())), preferred_element_type=F32)


def tn(a, b):
    return lax.dot_general(a, b, (((0,), (0,)), ((), ())), preferred_element_type=F32)


def moments(v):
    centred = v - jnp.mean(v, axis=-1, keepdims=True)
    rstd = lax.rsqrt(jnp.mean(centred * centred, axis=-1, keepdims=True) + 1e-06)
    return centred * rstd, rstd


def norm_back(grad, hat, rstd, gain):
    u = grad * gain
    return rstd * (
        u - jnp.mean(u, axis=-1, keepdims=True) - hat * jnp.mean(u * hat, axis=-1, keepdims=True)
    )


def row(ref):
    return ref[...].reshape(1, ref.shape[0])


def pack_kernel(wq, small, out):
    out[0:576, :] = wq[...]
    high = small[...].astype(BF)
    low = small[...] - high.astype(F32)
    out[576:592, :] = jnp.concatenate([high.astype(F32), low], axis=0).astype(BF)


def smalls(rows):
    both = rows.astype(F32)
    return both[0:8, :] + both[8:16, :]


def prep_kernel(
    me, lengths, left, mid, right, gain, bias, rows, cols, ct, scale_two, normed, extk, ohq, g_out
):
    scale, offset = row(gain), row(bias)
    at = 0
    for ref in (left, mid, right):
        for i in range(ref.shape[0] // 32):
            hat, _ = moments(ref[32 * i : 32 * i + 32, :].astype(F32))
            normed[at : at + 32, :] = (hat * scale + offset).astype(BF)
            at += 32

    for i in range(ct.shape[0] // 64):
        here = slice(64 * i, 64 * i + 64)
        g_out[here, :] = (row(scale_two) * ct[here, :].astype(F32)).astype(BF)

    own = mid.shape[0]
    tiles = rows.shape[0]
    first = me[0, 0] * (own // 128) - 2
    pick = lambda ref: jnp.concatenate([ref[pl.ds(jnp.clip(first + t, 0, tiles - 1), 1), :] for t in range(8)], axis=1)
    by_row, by_col = pick(rows), pick(cols)
    place = lax.broadcasted_iota(jnp.int32, (1, 1024), 1) + first * 128
    inside = (place >= 0) & (place < tiles * 128)
    page = jnp.zeros((1, 1024), jnp.int32)
    end = 0
    for i in range(lengths.shape[1]):
        end = end + lengths[0, i]
        page = page + jnp.where(place >= end, 1, 0)

    def hot(sub, row_at, col_at, bit_at, swapped):
        hit = (by_row == row_at) | (by_col == col_at)
        for b in range(4):
            bit = (page >> b) & 1
            hit = hit | ((sub == bit_at + 2 * b + swapped) & (bit == 0))
            hit = hit | ((sub == bit_at + 2 * b + 1 - swapped) & (bit == 1))
        return hit

    sub = lax.broadcasted_iota(jnp.int32, (64, 1024), 0)
    rest = jnp.where(sub < 28, sub, sub - 28)
    row_at = jnp.where((rest < GRID) & (sub < 56), GRID - 1 - rest, -1)
    col_at = jnp.where((rest >= GRID) & (sub < 56), 2 * GRID - 1 - rest, -1)
    keys = hot(sub, row_at, col_at, 56, 0) | ((sub >= 56) & jnp.logical_not(inside))
    keys = jnp.where(keys, 1.0, 0.0).T
    extk[...] = keys[256 - HALO : 256 + own + HALO, :].astype(BF)
    sub = lax.broadcasted_iota(jnp.int32, (128, 1024), 0)
    none = jnp.full((128, 1024), -1, jnp.int32)
    row_at = jnp.where(sub < GRID, GRID - 1 - sub, jnp.where((sub >= 64) & (sub < 64 + GRID), sub - 64, none))
    other = sub - 16
    col_at = jnp.where((other >= 0) & (other < GRID), GRID - 1 - other, none)
    col_at = jnp.where((sub >= 80) & (sub < 80 + GRID), sub - 80, col_at)
    queries = jnp.where(hot(sub, row_at, col_at, 32, 1), 1.0, 0.0)
    ohq[...] = queries[:, 256 : 256 + own].T.astype(BF)


def bias_table(rows, cols):
    lane = lax.broadcasted_iota(jnp.int32, (16, 128), 1)
    groups = []
    for table, first in ((rows, 64), (cols, 64 + GRID)):
        table = jnp.broadcast_to(table, (16, 128))
        high = table.astype(BF).astype(F32)
        total = jnp.zeros((16, 128), F32)
        for part, at in ((high, first), (table - high, first + 2 * GRID)):
            turned = pltpu.roll(part, (at - GRID + 1) % 128, 1, stride=1, stride_axis=0)
            total = total + jnp.where((lane >= at) & (lane < at + GRID), turned, 0.0)
        groups.append(total)
    lane = lax.broadcasted_iota(jnp.int32, (96, 128), 1)
    sub = lax.broadcasted_iota(jnp.int32, (96, 128), 0)
    bits = jnp.where((sub < 8) & (lane == sub + 120), -BIG, 0.0)
    return jnp.concatenate(groups + [bits], axis=0).astype(BF)


def attn_fwd_kernel(
    normed, w, extk, ohq, k_out, q_out, v_out, att_out, lse_out, tok, vt
):
    own = mid_rows = q_out.shape[1]
    tok[...] = jnp.zeros(tok.shape, F32)
    small = smalls(w[576:592, :])
    q = nt(normed[HALO : HALO + own, :], w[0:192, :]) + small[6:7, 0:192]
    q = q.astype(BF).astype(F32) * (HEAD_DIM**-0.5)
    q = jnp.concatenate([q, jnp.zeros((own, 64), F32)], axis=1)
    lane = lax.broadcasted_iota(jnp.int32, (own, 256), 1)
    for i in range(3):
        here = (lane >= 64 * i) & (lane < 64 * i + 64)
        ext = nn(ohq[...], bias_table(small[i : i + 1, 0:128], small[3 + i : 4 + i, 0:128]))
        ext = jnp.concatenate([jnp.zeros((own, 128), F32), ext], axis=1)
        q_out[i] = (jnp.where(here, q, 0.0) + ext).astype(BF)
    k = nt(normed[...], w[192:384, :]).astype(BF)
    k_out[...] = jnp.concatenate([k, extk[...]], axis=1)
    v = nt(normed[...], w[384:576, :]) + small[6:7, 256:448]
    v_out[...] = v.astype(BF)
    vt[...] = v.T.astype(BF)
    for b in range(mid_rows // QB):
        at = slice(b * QB, b * QB + WIN)
        here = slice(b * QB, b * QB + QB)
        parts = []
        keys = k_out[at, :]
        for i in range(3):
            s = nt(keys, q_out[i, here, :])
            top = jnp.max(s, axis=0, keepdims=True)
            e = jnp.exp(s - top)
            total = jnp.sum(e, axis=0, keepdims=True)
            o = nn(vt[64 * i : 64 * i + 64, at], e.astype(BF))
            parts.append(o / total)
            lse_out[i : i + 1, here] = top + jnp.log(total)
        att_out[here, :] = jnp.concatenate(parts, axis=0).T.astype(BF)


def mid_kernel(
    a0, a1, a2, a3, w0, w1, w2, w3, x, b_out, scale, gain, bias, branch_out, mid_out, n2_first, n2_second
):
    step = 128
    for i in range(x.shape[0] // step):
        at = slice(i * step, (i + 1) * step)
        branch = nn(a0[at, :], w0[...]) + nn(a1[at, :], w1[...])
        branch = branch + nn(a2[at, :], w2[...]) + nn(a3[at, :], w3[...])
        branch = branch + row(b_out)
        middle = x[at, :].astype(F32) + row(scale) * branch
        hat, _ = moments(middle)
        branch_out[at, :] = branch
        mid_out[at, :] = middle
        out = (n2_first, n2_second)[i // 2]
        here = i % 2 * step
        out[here : here + step, :] = (hat * row(gain) + row(bias)).astype(BF)


def mlp_kernel(chunks, first, *refs):
    n2 = refs[:chunks]
    g, wu0, wd0, wu1, wd1, s0, s1, act0, act1, dpre0, dpre1, b_out, n_out, sums = refs[chunks:]
    c = 0.7978845608028654
    step = 256
    totals = []
    for wu, wd, s, act, dpre, r in ((wu0, wd0, s0, act0, dpre0, 0), (wu1, wd1, s1, act1, dpre1, 1)):
        bias = smalls(s[...])[7:8, :]
        total = jnp.zeros((1, wu.shape[1]), F32)
        for i in range(chunks):
            at = slice(i * step, (i + 1) * step)
            pre = nn(n2[i][...], wu[...]) + bias
            sq = pre * pre
            t = jnp.tanh(c * pre * (1.0 + 0.044715 * sq))
            half = 0.5 * (1.0 + t)
            slope = half + (0.5 * c) * pre * (1.0 - t * t) * (1.0 + (3 * 0.044715) * sq)
            a = (pre * half).astype(BF)
            act[at, :] = a
            dp = (nt(g[first + i * step : first + (i + 1) * step, :], wd[...]) * slope).astype(BF)
            dpre[at, :] = dp
            total = total + jnp.sum(dp.astype(F32), axis=0, keepdims=True)
        totals.append(total)
    for i in range(chunks):
        at = slice(i * step, (i + 1) * step)
        n_out[at, :] = (nt(dpre0[at, :], wu0[...]) + nt(dpre1[at, :], wu1[...])).astype(n_out.dtype)
        b_out[at, :] = (nn(act0[at, :], wd0[...]) + nn(act1[at, :], wd1[...])).astype(b_out.dtype)
    sums[...] = jnp.concatenate(totals + [jnp.zeros((6, 768), F32)], axis=0)


def weights_kernel(
    r, n2a, n2b, n2c, n2d, g, g_far, act, act_c, act_d, dpre, dpre_c, dpre_d, sa, sb, sc, sums, *outs
):
    rows = lambda *parts: jnp.concatenate([p[...] for p in parts], axis=0)
    up = tn(rows(n2a, n2b, n2c, n2d), rows(dpre, dpre_c, dpre_d)).astype(BF)
    down = tn(rows(act, act_c, act_d), rows(g, g_far)).astype(BF)
    for i in range(4):
        outs[i][...] = up[192 * i : 192 * i + 192, :]
        outs[4 + i][...] = down[192 * i : 192 * i + 192, :]
    line = sa[r : r + 1, :] + sb[r : r + 1, :] + sc[r : r + 1, :]
    sums[...] = jnp.broadcast_to(line, sums.shape)


def midb_kernel(mid, branch, ct, gn2, ret_a, ret_b, gain, scale, mg_out, gb_out, sums):
    step = 64
    acc = [jnp.zeros((1, mid.shape[1]), F32)] * 4
    for i in range(mid.shape[0] // step):
        at = slice(i * step, (i + 1) * step)
        ret, here = ((ret_a, i * step), (ret_b, i * step - 256))[i * step // 256]
        hat, rstd = moments(mid[at, :])
        g = gn2[at, :] + ret[here : here + step, :].astype(F32)
        mg = ct[at, :].astype(F32) + norm_back(g, hat, rstd, row(gain))
        mg_out[at, :] = mg
        gb = row(scale) * mg
        gb_out[at, :] = gb.astype(BF)
        terms = [gb, mg * branch[at, :], g * hat, g]
        acc = [a + jnp.sum(t, axis=0, keepdims=True) for a, t in zip(acc, terms)]
    sums[...] = jnp.concatenate(acc + [jnp.zeros((4, mid.shape[1]), F32)], axis=0)


def attn_bwd_kernel(
    k, q, v, lse, gb, w, wo, att, ohq, normed, up_sum, acc,
    g_first, g_last, acc_out, small_out, kt, dkacc, dvacc, do, dqs,
):
    own = q.shape[1]
    mine = slice(HALO, HALO + own)
    g_last[192:384, :] = tn(att[...], gb[...]).astype(BF)
    do[...] = nt(gb[...], wo[...]).astype(BF)
    kt[...] = k[...].astype(F32).T.astype(BF)
    dkacc[...] = jnp.zeros(dkacc.shape, F32)
    dvacc[...] = jnp.zeros(dvacc.shape, F32)
    lane = lax.broadcasted_iota(jnp.int32, (QB, 192), 1)
    rel = jnp.zeros((192, 128), F32)
    for b in range(own // QB):
        at = slice(b * QB, b * QB + WIN)
        here = slice(b * QB, b * QB + QB)
        keys = k[at, :]
        vals = v[at, :]
        d_block = do[here, :]
        dk, dv = dkacc[at, :], dvacc[at, :]
        qparts, lparts = [], []
        for i in range(3):
            qb = q[i, here, :]
            s = nt(keys, qb)
            p = jnp.exp(s - lse[i : i + 1, here])
            head = (lane >= 64 * i) & (lane < 64 * i + 64)
            db = jnp.where(head, d_block, jnp.zeros_like(d_block))
            dp = nt(vals, db)
            inner = jnp.sum(p * dp, axis=0, keepdims=True)
            ds = (p * (dp - inner)).astype(BF)
            dv = dv + nn(p.astype(BF), db)
            dk = dk + nn(ds, qb)
            qparts.append(nn(kt[64 * i : 64 * i + 64, at], ds))
            lparts.append(nn(kt[192:256, at], ds))
        dkacc[at, :] = dk
        dvacc[at, :] = dv
        dq = jnp.concatenate(qparts, axis=0) * (HEAD_DIM**-0.5)
        dqs[here, :] = dq.T.astype(BF)
        lift = jnp.concatenate(lparts, axis=0)
        high = lift.astype(BF)
        low = (lift - high.astype(F32)).astype(BF)
        rel = rel + nn(high, ohq[here, :]) + nn(low, ohq[here, :])
    dk = dkacc[:, 0:192].astype(BF)
    dv = dvacc[...].astype(BF)
    g_first[0:192, :] = tn(dqs[...], normed[mine, :]).astype(BF)
    g_first[192:384, :] = tn(dk, normed[...]).astype(BF)
    g_last[0:192, :] = tn(dv, normed[...]).astype(BF)
    acc_out[...] = acc[...] + nn(dk, w[192:384, :]) + nn(dv, w[384:576, :])
    acc_out[mine, :] += nn(dqs[...], w[0:192, :])
    lane = lax.broadcasted_iota(jnp.int32, (16, 128), 1)
    sub = lax.broadcasted_iota(jnp.int32, (16, 128), 0)
    lane_c = lax.broadcasted_iota(jnp.int32, (24, 128), 1)
    sub_c = lax.broadcasted_iota(jnp.int32, (24, 128), 0)
    by_row, by_col = [], []
    for i in range(3):
        part = jnp.where((sub < GRID) & (lane >= 64) & (lane < 64 + GRID), rel[64 * i : 64 * i + 16, :], 0.0)
        part = pltpu.roll(part, 0, 1, stride=1, stride_axis=0)
        by_row.append(jnp.sum(part, axis=0, keepdims=True))
        keep = (sub_c >= 6) & (sub_c < 6 + GRID) & (lane_c >= 80) & (lane_c < 80 + GRID)
        part = jnp.where(keep, rel[64 * i + 8 : 64 * i + 32, :], 0.0)
        part = pltpu.roll(part, 0, 1, stride=1, stride_axis=0)
        by_col.append(jnp.sum(part, axis=0, keepdims=True))
    sums = [jnp.sum(t.astype(F32), axis=0, keepdims=True) for t in (dqs[...], dv)]
    rels = jnp.concatenate(by_row + by_col, axis=0)
    small_out[0:6, :] = jnp.concatenate([rels, jnp.zeros((6, 640), F32)], axis=1)
    none = jnp.zeros((1, 64), F32)
    small_out[6:7, :] = jnp.concatenate([sums[0], none, sums[1], none, jnp.zeros((1, 256), F32)], axis=1)
    small_out[7:8, :] = up_sum[0:1, :]


def out_kernel(mid, two, ret_a, ret_b, ct, b_down, scale_two, before, lo_out, sums):
    step = 64
    acc = [jnp.zeros((1, mid.shape[1]), F32)] * 2
    for i in range(mid.shape[0] // step):
        at = slice(i * step, (i + 1) * step)
        ret, here = ((ret_a, i * step), (ret_b, i * step - 256))[i * step // 256]
        branch_two = two[at, :] + ret[here : here + step, :].astype(F32) + row(b_down)
        lo_out[at, :] = (mid[at, :] + row(scale_two) * branch_two).astype(BF)
        up = ct[at, :].astype(F32)
        terms = [row(scale_two) * up, up * branch_two]
        acc = [a + jnp.sum(t, axis=0, keepdims=True) for a, t in zip(acc, terms)]
    sums[...] = jnp.concatenate([before[0:4, :]] + acc + [before[6:8, :]], axis=0)


def sums_kernel(left, mid, right, acc, before, sums):
    total = [jnp.zeros((1, acc.shape[1]), F32)] * 2
    at = 0
    for ref in (left, mid, right):
        for i in range(ref.shape[0] // 32):
            hat, _ = moments(ref[32 * i : 32 * i + 32, :].astype(F32))
            g = acc[at : at + 32, :]
            total = [t + jnp.sum(v, axis=0, keepdims=True) for t, v in zip(total, [g * hat, g])]
            at += 32
    sums[...] = jnp.concatenate([before[0:6, :]] + total, axis=0)


def final_kernel(x, gn1, fl, fr, mg, gain, in_out):
    step = 32
    own = x.shape[0]
    for i in range(own // step):
        at = slice(i * step, (i + 1) * step)
        hat, rstd = moments(x[at, :].astype(F32))
        g = gn1[HALO + i * step : HALO + (i + 1) * step, :]
        if (i + 1) * step <= HALO:
            g = g + fl[at, :].astype(F32)
        tail = i * step - (own - HALO)
        if tail >= 0:
            g = g + fr[tail : tail + step, :].astype(F32)
        in_out[at, :] = mg[at, :] + norm_back(g, hat, rstd, row(gain))


def unpack_kernel(sums, b_up, b_qv, rel_row, rel_col, *wholes):
    total = sums[...].astype(F32)
    b_up[...] = total[7:8, :].reshape(768)
    b_qv[...] = jnp.concatenate([total[6:7, 0:192], total[6:7, 256:448]], axis=0)
    rel_row[...] = total[0:3, 64:91]
    rel_col[...] = total[3:6, 86:113]
    for i, out in enumerate(wholes):
        out[...] = total[8 + i : 9 + i, :].reshape(768)


def op(kernel, outs, args, specs=None, out_specs=None, scratch=(), aliases=None, limit=18, after=()):
    n = len(args)

    def body(*refs):
        kernel(*refs[:n], *refs[n + len(after) :])

    return pl.pallas_call(
        body,
        out_shape=[jax.ShapeDtypeStruct(s, d) for s, d in outs],
        in_specs=(specs or [VMEM] * n) + [pl.BlockSpec(memory_space=pl.ANY)] * len(after),
        out_specs=out_specs or [VMEM] * len(outs),
        scratch_shapes=list(scratch),
        compiler_params=pltpu.CompilerParams(vmem_limit_bytes=limit * MIB),
        input_output_aliases=aliases or {},
    )(*args, *after)


VMEM = pl.BlockSpec(memory_space=pltpu.VMEM)
SMEM = pl.BlockSpec(memory_space=pltpu.SMEM)


def behind(v, first):
    if v.shape[-1] != first.shape[-1]:
        return v
    return jnp.where(first[0:1].astype(F32) > 3e38, jnp.zeros_like(v), v)


def add(*parts):
    return sum(p.astype(F32) for p in parts).astype(BF)


def halves(v, bit):
    n = v.shape[0] // 2
    return [jnp.where(bit == 0, v[:n], v[n:]), jnp.where(bit == 0, v[n:], v[:n])]


def joined(mine, other, bit):
    return jnp.concatenate([jnp.where(bit == 0, mine, other), jnp.where(bit == 0, other, mine)], axis=0)


def send(v, axis, pairs):
    return lax.ppermute(v, axis, pairs)


def make_body(ndp, nmp):
    assert nmp == 4 and ndp % 8 == 0 and ndp & (ndp - 1) == 0
    core = ("mp", [(i, i ^ 1) for i in range(nmp)])
    over_y = ("mp", [(i, i ^ 2) for i in range(nmp)])
    over_x = ("dp", [(i, i ^ 1) for i in range(ndp)])
    over_four = [("dp", [(i, i ^ b) for i in range(ndp)]) for b in (2, 1, 3)]
    over_far = [("dp", [(i, i ^ (1 << b)) for i in range(ndp)]) for b in range(2, ndp.bit_length() - 1)]
    rightward = ("mp", [(i, i + 1) for i in range(nmp - 1)])
    leftward = ("mp", [(i + 1, i) for i in range(nmp - 1)])

    def body(
        layer_in, ln1_gain, ln1_bias, w_qkv, b_qv, rel_row, rel_col, w_out, b_out, scale_attn, ln2_gain,
        ln2_bias, w_up, b_up, w_down, b_down, scale_mlp, page_lengths, patch_rows, patch_cols, cotangent,
    ):
        own, width = layer_in.shape
        kv = own + 2 * HALO
        units = w_up.shape[1]
        cols = w_qkv.shape[2]
        me = lax.axis_index("mp")
        x_bit = lax.axis_index("dp") & 1
        z_bit = (lax.axis_index("dp") >> 1) & 1
        line = ((8, width), F32)

        left, right = send(layer_in[own - HALO :], *rightward), send(layer_in[:HALO], *leftward)
        wq = jnp.transpose(w_qkv, (0, 2, 1)).reshape(3 * cols, width)
        place = lambda v, at, lane: jnp.pad(v, ((at, 8 - at - v.shape[0]), (lane, width - lane - v.shape[1])))
        small = place(rel_row, 0, 0) + place(rel_col, 3, 0) + place(b_up[None], 7, 0)
        small = small + place(b_qv[0:1], 6, 0) + place(b_qv[1:2], 6, 256)
        (packed,) = op(pack_kernel, [((3 * cols + 16, width), BF)], [wq, small])
        mine = jnp.split(halves(packed, x_bit)[0], 2, axis=0)
        packed_y = [send(v, *over_y) for v in mine]
        packed_near = send(packed, *core)
        out_y, out_near = send(w_out, *over_y), send(w_out, *core)
        up_near, down_near = send(w_up, *core), send(w_down, *core)
        normed, extk, ohq, mlp_grad = op(
            prep_kernel, [((kv, width), BF), ((kv, 64), BF), ((own, 128), BF), ((own, width), BF)],
            [
                me.reshape(1, 1), page_lengths, left, layer_in, right, ln1_gain, ln1_bias,
                patch_rows.reshape(-1, 128), patch_cols.reshape(-1, 128), cotangent, scale_mlp,
            ],
            specs=[SMEM, SMEM] + [VMEM] * 9, after=mine,
        )
        mlp_grad_y = send(mlp_grad, *over_y)

        def attention(w, after=()):
            outs = [((kv, 256), BF), ((3, own, 256), BF), ((kv, 192), BF), ((own, 192), BF), ((8, own), F32), line]
            return op(
                attn_fwd_kernel, outs, [normed, w, extk, ohq], scratch=[pltpu.VMEM((192, kv), BF)], after=after
            )

        fwd = [attention(packed)]
        packed_y = [behind(v, fwd[0][5]) for v in packed_y]
        packed_x = [send(v, *over_x) for v in packed_y]
        fwd.append(attention(packed_near, after=packed_y))
        packed_x = [behind(v, fwd[1][5]) for v in packed_x]
        packed_far = joined(jnp.concatenate(packed_y, axis=0), jnp.concatenate(packed_x, axis=0), x_bit)
        packed_diag = jnp.concatenate([send(packed_far[:304], *core), send(packed_far[304:], *core)], axis=0)
        fwd.append(attention(packed_far))
        out_far = behind(out_y, fwd[2][5])
        out_diag = send(out_far, *core)
        fwd.append(attention(packed_diag, after=[out_far]))
        ins_w, outs_w = [packed, packed_near, packed_far, packed_diag], [w_out, out_near, out_far, out_diag]
        part = ((own // 2, width), BF)
        branch, middle, n2a, n2b = op(
            mid_kernel, [((own, width), F32), ((own, width), F32), part, part],
            [*[f[3] for f in fwd], *outs_w, layer_in, b_out, scale_attn, ln2_gain, ln2_bias], after=[mlp_grad_y],
        )

        n2c, n2d = send(n2a, *over_y), send(n2b, *over_y)
        tails = [w[3 * cols :] for w in ins_w[:2]]

        def mlp(n2, g, first, dtype, after=()):
            rows = len(n2) * n2[0].shape[0]
            return op(
                functools.partial(mlp_kernel, len(n2), first),
                [((rows, units), BF)] * 4 + [((rows, width), dtype)] * 2 + [line],
                [*n2, g, w_up, w_down, up_near, down_near, *tails], after=after,
            )

        mine_mlp = mlp([n2a, n2b], mlp_grad, 0, F32)
        first_mlp = mlp([n2c], mlp_grad_y, 0, BF, after=[mine_mlp[6]])
        ret_na, ret_ba = send(first_mlp[5], *over_y), send(first_mlp[4], *over_y)
        second_mlp = mlp([n2d], mlp_grad_y, own // 2, BF, after=[first_mlp[6]])
        ret_nb, ret_bb = send(second_mlp[5], *over_y), send(second_mlp[4], *over_y)

        def weights(r, after):
            parts = [mine_mlp, first_mlp, second_mlp]
            return op(
                functools.partial(weights_kernel, r), [line] + [((width // 4, width), BF)] * 8,
                [
                    n2a, n2b, n2c, n2d, mlp_grad, mlp_grad_y, *[p[r] for p in parts], *[p[2 + r] for p in parts],
                    *[p[6] for p in parts],
                ],
                after=after,
            )

        up_far_sum, *grads_far = weights(1, [second_mlp[6], ret_na])
        mlp_near = [send(g, *core) for g in grads_far]
        up_own_sum, *grads_own = weights(0, [up_far_sum])
        up_sums = [up_own_sum, up_far_sum] + [jnp.zeros((8, width), F32)] * 2
        middle_grad, branch_grad, sums_two = op(
            midb_kernel, [((own, width), F32), ((own, width), BF), line],
            [middle, branch, cotangent, mine_mlp[5], ret_na, ret_nb, ln2_gain, scale_attn], after=[up_own_sum],
        )

        results, asked = {}, {}

        def four(v):
            mine, other = halves(v, x_bit)
            return halves(mine, z_bit) + halves(other, z_bit)

        def whole_of(own, z, x, both):
            return joined(joined(own, z, z_bit), joined(x, both, z_bit), x_bit)

        def pairs(own, z, x, both):
            return add(add(own, z).astype(F32), add(x, both).astype(F32)).astype(BF)

        def long_block(name, near):
            keep, other = yield lambda *p: halves(add(*p), x_bit), near
            there = send(other, *over_four[1])
            keep, other = yield lambda a, b: halves(add(a, b), z_bit), [keep, there]
            there = send(other, *over_four[0])
            for link in over_far:
                (keep,) = yield lambda a, b: [add(a, b)], [keep, there]
                there = send(keep, *link)
            (keep,) = yield lambda a, b: [add(a, b)], [keep, there]
            there = send(keep, *over_four[0])
            (keep,) = yield lambda a, b: [joined(a, b, z_bit)], [keep, there]
            there = send(keep, *over_four[1])
            (results[name],) = yield lambda a, b: [joined(a, b, x_bit)], [keep, there]

        def block(name, near, far=None, extra=None):
            there = [send(far, *over_y)] if far is not None else []
            keep, *others = yield lambda *p: four(add(*p)), lambda: near() + there
            there = [send(v, *link) for v, link in zip(others, over_four)]
            (keep,) = yield lambda *v: [add(*v)], [keep, *there]
            if extra:
                keep = jnp.concatenate([keep, extra[0].astype(BF)], axis=0)
            for link in over_far:
                there = send(keep, *link)
                (keep,) = yield lambda a, b: [add(a, b)], [keep, there]
            there = [send(keep, *link) for link in over_four]
            n = width // 4
            whole, *small = yield (
                lambda *v: [whole_of(*[p[:n] for p in v])] + ([pairs(*[p[n:] for p in v])] if extra else []),
                [keep, *there],
            )
            results[name] = whole
            if extra:
                flat = ((width,), F32)
                results["small"] = op(
                    unpack_kernel, [flat, ((2, 192), F32), ((3, 27), F32), ((3, 27), F32)] + [flat] * 8, small
                )

        def start(flow):
            asked[flow] = next(flow)
            return flow

        def steps(first, *flows):
            flows = [f for f in flows if f in asked]
            wanted = [(fn, args() if callable(args) else args) for fn, args in (asked.pop(f) for f in flows)]
            *given, at = lax.optimization_barrier((*[a for _, args in wanted for a in args], first))
            made, counts = [], []
            for fn, args in wanted:
                outs = fn(*[behind(a, at) for a in given[: len(args)]])
                given = given[len(args) :]
                made += outs
                counts.append(len(outs))
            outs = made = list(lax.optimization_barrier(made))
            for flow, count in zip(flows, counts):
                try:
                    asked[flow] = flow.send(outs[:count])
                except StopIteration:
                    pass
                outs = outs[count:]
            return [m for m in made if m.shape[-1] == width]

        whole = lambda parts: jnp.concatenate(parts, axis=0)
        up_flow = start(long_block("up", lambda: [whole(grads_own[:4]), whole(mlp_near[:4])]))
        down_flow = start(long_block("down", lambda: [whole(grads_own[4:]), whole(mlp_near[4:])]))
        made = steps(sums_two, up_flow, down_flow)

        grads_att, tiny, acc = [None] * 4, [None] * 4, jnp.zeros((kv, width), F32)
        n = width // 2

        def attention_back(r, acc, after=()):
            k, q, v, att, lse, _ = fwd[r]
            *grads_att[r], acc, tiny[r] = op(
                attn_bwd_kernel, [((n, width), BF), ((n, width), BF), ((kv, width), F32), line],
                [k, q, v, lse, branch_grad, ins_w[r], outs_w[r], att, ohq, normed, up_sums[r], acc],
                scratch=[
                    pltpu.VMEM((256, kv), BF), pltpu.VMEM((kv, 256), F32), pltpu.VMEM((kv, 192), F32),
                    pltpu.VMEM((own, 192), BF), pltpu.VMEM((own, 192), BF),
                ],
                aliases={11: 2}, after=after,
            )
            return acc

        acc = attention_back(3, acc, after=made)
        att_far = [send(g, *core) for g in grads_att[3]]
        made = steps(grads_att[3][0], up_flow)
        layer_out, sums_out = op(
            out_kernel, [((own, width), BF), line],
            [middle, mine_mlp[4], ret_ba, ret_bb, cotangent, b_down, scale_mlp, sums_two], after=[grads_att[3][0]],
        )
        acc = attention_back(2, acc, after=[sums_out, *made])
        far_sums = [add(a, behind(b, grads_att[2][0])) for a, b in zip(grads_att[2], att_far)]
        att_near, extra = [], []
        att_flow = start(block("att", lambda: [whole(grads_att[0]), whole(att_near)], whole(far_sums), extra))
        made = steps(grads_att[2][0], up_flow, down_flow)
        acc = attention_back(1, acc, after=[*made, *far_sums])
        att_near += [send(g, *core) for g in grads_att[1]]
        made = steps(grads_att[1][0], up_flow, down_flow)
        acc = attention_back(0, acc, after=made)
        to_left, to_right = acc[:HALO].astype(BF), acc[HALO + own :].astype(BF)
        from_left, from_right = send(to_right, *rightward), send(to_left, *leftward)

        made = steps(grads_att[0][0], att_flow, up_flow, down_flow)

        (sums_in,) = op(sums_kernel, [line], [left, layer_in, right, acc, sums_out], after=made[:1])
        there = send(jnp.concatenate([tiny[1], sums_in, tiny[3], sums_in], axis=0), *core)
        near_small = jnp.concatenate([tiny[0], sums_in], axis=0) + there[:16]
        far_small = jnp.concatenate([tiny[2], sums_in], axis=0) + there[16:]
        extra.append(near_small + send(far_small, *over_y))

        (input_grad,) = op(
            final_kernel, [((own, width), F32)], [layer_in, acc, from_left, from_right, middle_grad, ln1_gain],
            after=[sums_in],
        )
        while asked:
            made = steps(made[-1], *list(asked)) or made

        w_up_grad, w_down_grad = results["up"].astype(F32), results["down"].astype(F32)
        w_qkv_grad = results["att"][: 3 * cols].astype(F32)
        w_qkv_grad = jnp.transpose(w_qkv_grad.reshape(3, cols, width), (0, 2, 1))
        b_up_g, b_qv_g, rel_row_g, rel_col_g, *wholes = results["small"]
        b_out_g, scale_attn_g, ln2_gain_g, ln2_bias_g, b_down_g, scale_mlp_g, ln1_gain_g, ln1_bias_g = wholes
        return (
            layer_out, input_grad, ln1_gain_g, ln1_bias_g, w_qkv_grad, b_qv_g, rel_row_g, rel_col_g,
            results["att"][3 * cols :].astype(F32), b_out_g, scale_attn_g, ln2_gain_g, ln2_bias_g, w_up_grad, b_up_g, w_down_grad,
            b_down_g, scale_mlp_g,
        )

    return body


def solution(mesh):
    rows = P(("dp", "mp"), None)
    return jax.shard_map(
        make_body(mesh.shape["dp"], mesh.shape["mp"]),
        mesh=mesh,
        in_specs=(
            rows, P(), P(), P(None, None, "mp"), P(None, "mp"), P("mp", None), P("mp", None), P("mp", None),
            P(), P(), P(), P(), P(None, "mp"), P("mp"), P("mp", None), P(), P(), P("dp", None), P("dp"),
            P("dp"), rows,
        ),
        out_specs=(
            rows, rows, P(), P(), P(None, None, "mp"), P(None, "mp"), P("mp", None), P("mp", None),
            P("mp", None), P(), P(), P(), P(), P(None, "mp"), P("mp"), P("mp", None), P(), P(),
        ),
        check_vma=False,
    )
```

```python
import functools

import jax
import jax.numpy as jnp
import numpy as np
from jax import lax
from jax.experimental import pallas as pl
from jax.experimental.pallas import tpu as pltpu
from jax.sharding import PartitionSpec as P

HEAD_DIM = 64
GRID = 14
HALO = 160
QB = 128
WIN = QB + 2 * HALO
BIG = float(2**30)
F32 = jnp.float32
BF = jnp.bfloat16
MIB = 1024 * 1024


def nn(a, b):
    return lax.dot_general(a, b, (((1,), (0,)), ((), ())), preferred_element_type=F32)


def nt(a, b):
    return lax.dot_general(a, b, (((1,), (1,)), ((), ())), preferred_element_type=F32)


def tn(a, b):
    return lax.dot_general(a, b, (((0,), (0,)), ((), ())), preferred_element_type=F32)


def moments(v):
    centred = v - jnp.mean(v, axis=-1, keepdims=True)
    rstd = lax.rsqrt(jnp.mean(centred * centred, axis=-1, keepdims=True) + 1e-06)
    return centred * rstd, rstd


def norm_back(grad, hat, rstd, gain):
    u = grad * gain
    return rstd * (
        u - jnp.mean(u, axis=-1, keepdims=True) - hat * jnp.mean(u * hat, axis=-1, keepdims=True)
    )


def row(ref):
    return ref[...].reshape(1, ref.shape[0])


def pack_kernel(wq, small, out):
    out[0:576, :] = wq[...]
    high = small[...].astype(BF)
    low = small[...] - high.astype(F32)
    out[576:592, :] = jnp.concatenate([high.astype(F32), low], axis=0).astype(BF)


def smalls(rows):
    both = rows.astype(F32)
    return both[0:8, :] + both[8:16, :]


def prep_kernel(
    me, lengths, left, mid, right, gain, bias, rows, cols, ct, scale_two, normed, extk, ohq, g_out
):
    scale, offset = row(gain), row(bias)
    at = 0
    for ref in (left, mid, right):
        for i in range(ref.shape[0] // 32):
            hat, _ = moments(ref[32 * i : 32 * i + 32, :].astype(F32))
            normed[at : at + 32, :] = (hat * scale + offset).astype(BF)
            at += 32

    for i in range(ct.shape[0] // 64):
        here = slice(64 * i, 64 * i + 64)
        g_out[here, :] = (row(scale_two) * ct[here, :].astype(F32)).astype(BF)

    own = mid.shape[0]
    tiles = rows.shape[0]
    first = me[0, 0] * (own // 128) - 2
    pick = lambda ref: jnp.concatenate([ref[pl.ds(jnp.clip(first + t, 0, tiles - 1), 1), :] for t in range(8)], axis=1)
    by_row, by_col = pick(rows), pick(cols)
    place = lax.broadcasted_iota(jnp.int32, (1, 1024), 1) + first * 128
    inside = (place >= 0) & (place < tiles * 128)
    page = jnp.zeros((1, 1024), jnp.int32)
    end = 0
    for i in range(lengths.shape[1]):
        end = end + lengths[0, i]
        page = page + jnp.where(place >= end, 1, 0)

    def hot(sub, row_at, col_at, bit_at, swapped):
        hit = (by_row == row_at) | (by_col == col_at)
        for b in range(4):
            bit = (page >> b) & 1
            hit = hit | ((sub == bit_at + 2 * b + swapped) & (bit == 0))
            hit = hit | ((sub == bit_at + 2 * b + 1 - swapped) & (bit == 1))
        return hit

    sub = lax.broadcasted_iota(jnp.int32, (64, 1024), 0)
    rest = jnp.where(sub < 28, sub, sub - 28)
    row_at = jnp.where((rest < GRID) & (sub < 56), GRID - 1 - rest, -1)
    col_at = jnp.where((rest >= GRID) & (sub < 56), 2 * GRID - 1 - rest, -1)
    keys = hot(sub, row_at, col_at, 56, 0) | ((sub >= 56) & jnp.logical_not(inside))
    keys = jnp.where(keys, 1.0, 0.0).T
    extk[...] = keys[256 - HALO : 256 + own + HALO, :].astype(BF)
    sub = lax.broadcasted_iota(jnp.int32, (128, 1024), 0)
    none = jnp.full((128, 1024), -1, jnp.int32)
    row_at = jnp.where(sub < GRID, GRID - 1 - sub, jnp.where((sub >= 64) & (sub < 64 + GRID), sub - 64, none))
    other = sub - 16
    col_at = jnp.where((other >= 0) & (other < GRID), GRID - 1 - other, none)
    col_at = jnp.where((sub >= 80) & (sub < 80 + GRID), sub - 80, col_at)
    queries = jnp.where(hot(sub, row_at, col_at, 32, 1), 1.0, 0.0)
    ohq[...] = queries[:, 256 : 256 + own].T.astype(BF)


def bias_table(rows, cols):
    lane = lax.broadcasted_iota(jnp.int32, (16, 128), 1)
    groups = []
    for table, first in ((rows, 64), (cols, 64 + GRID)):
        table = jnp.broadcast_to(table, (16, 128))
        high = table.astype(BF).astype(F32)
        total = jnp.zeros((16, 128), F32)
        for part, at in ((high, first), (table - high, first + 2 * GRID)):
            turned = pltpu.roll(part, (at - GRID + 1) % 128, 1, stride=1, stride_axis=0)
            total = total + jnp.where((lane >= at) & (lane < at + GRID), turned, 0.0)
        groups.append(total)
    lane = lax.broadcasted_iota(jnp.int32, (96, 128), 1)
    sub = lax.broadcasted_iota(jnp.int32, (96, 128), 0)
    bits = jnp.where((sub < 8) & (lane == sub + 120), -BIG, 0.0)
    return jnp.concatenate(groups + [bits], axis=0).astype(BF)


def attn_fwd_kernel(
    normed, w, extk, ohq, k_out, q_out, v_out, att_out, lse_out, tok, vt
):
    own = mid_rows = q_out.shape[1]
    tok[...] = jnp.zeros(tok.shape, F32)
    small = smalls(w[576:592, :])
    q = nt(normed[HALO : HALO + own, :], w[0:192, :]) + small[6:7, 0:192]
    q = q.astype(BF).astype(F32) * (HEAD_DIM**-0.5)
    q = jnp.concatenate([q, jnp.zeros((own, 64), F32)], axis=1)
    lane = lax.broadcasted_iota(jnp.int32, (own, 256), 1)
    for i in range(3):
        here = (lane >= 64 * i) & (lane < 64 * i + 64)
        ext = nn(ohq[...], bias_table(small[i : i + 1, 0:128], small[3 + i : 4 + i, 0:128]))
        ext = jnp.concatenate([jnp.zeros((own, 128), F32), ext], axis=1)
        q_out[i] = (jnp.where(here, q, 0.0) + ext).astype(BF)
    k = nt(normed[...], w[192:384, :]).astype(BF)
    k_out[...] = jnp.concatenate([k, extk[...]], axis=1)
    v = nt(normed[...], w[384:576, :]) + small[6:7, 256:448]
    v_out[...] = v.astype(BF)
    vt[...] = v.T.astype(BF)
    for b in range(mid_rows // QB):
        at = slice(b * QB, b * QB + WIN)
        here = slice(b * QB, b * QB + QB)
        queries = jnp.concatenate([q_out[i, here, :] for i in range(3)], axis=0)
        scores = nt(k_out[at, :], queries)
        top = jnp.max(scores, axis=0, keepdims=True)
        e = jnp.exp(scores - top)
        total = jnp.sum(e, axis=0, keepdims=True)
        e = e.astype(BF)
        lse = top + jnp.log(total)
        parts = []
        for i in range(3):
            cols = slice(QB * i, QB * i + QB)
            parts.append(nn(vt[64 * i : 64 * i + 64, at], e[:, cols]) / total[:, cols])
            lse_out[i : i + 1, here] = lse[:, cols]
        att_out[here, :] = jnp.concatenate(parts, axis=0).T.astype(BF)


def mid_kernel(
    a0, a1, a2, a3, w0, w1, w2, w3, x, b_out, scale, gain, bias, branch_out, mid_out, n2_first, n2_second
):
    step = 128
    for i in range(x.shape[0] // step):
        at = slice(i * step, (i + 1) * step)
        branch = nn(a0[at, :], w0[...]) + nn(a1[at, :], w1[...])
        branch = branch + nn(a2[at, :], w2[...]) + nn(a3[at, :], w3[...])
        branch = branch + row(b_out)
        middle = x[at, :].astype(F32) + row(scale) * branch
        hat, _ = moments(middle)
        branch_out[at, :] = branch
        mid_out[at, :] = middle
        out = (n2_first, n2_second)[i // 2]
        here = i % 2 * step
        out[here : here + step, :] = (hat * row(gain) + row(bias)).astype(BF)


def mlp_kernel(chunks, first, *refs):
    n2 = refs[:chunks]
    g, wu0, wd0, wu1, wd1, s0, s1, act0, act1, dpre0, dpre1, b_out, n_out, sums = refs[chunks:]
    c = 0.7978845608028654
    step = 256
    totals = []
    for wu, wd, s, act, dpre, r in ((wu0, wd0, s0, act0, dpre0, 0), (wu1, wd1, s1, act1, dpre1, 1)):
        bias = smalls(s[...])[7:8, :]
        total = jnp.zeros((1, wu.shape[1]), F32)
        for i in range(chunks):
            at = slice(i * step, (i + 1) * step)
            pre = nn(n2[i][...], wu[...]) + bias
            sq = pre * pre
            t = jnp.tanh(c * pre * (1.0 + 0.044715 * sq))
            half = 0.5 * (1.0 + t)
            slope = half + (0.5 * c) * pre * (1.0 - t * t) * (1.0 + (3 * 0.044715) * sq)
            a = (pre * half).astype(BF)
            act[at, :] = a
            dp = (nt(g[first + i * step : first + (i + 1) * step, :], wd[...]) * slope).astype(BF)
            dpre[at, :] = dp
            total = total + jnp.sum(dp.astype(F32), axis=0, keepdims=True)
        totals.append(total)
    for i in range(chunks):
        at = slice(i * step, (i + 1) * step)
        n_out[at, :] = (nt(dpre0[at, :], wu0[...]) + nt(dpre1[at, :], wu1[...])).astype(n_out.dtype)
        b_out[at, :] = (nn(act0[at, :], wd0[...]) + nn(act1[at, :], wd1[...])).astype(b_out.dtype)
    sums[...] = jnp.concatenate(totals + [jnp.zeros((6, 768), F32)], axis=0)


def weights_kernel(
    r, n2a, n2b, n2c, n2d, g, g_far, act, act_c, act_d, dpre, dpre_c, dpre_d, sa, sb, sc, sums, *outs
):
    rows = lambda *parts: jnp.concatenate([p[...] for p in parts], axis=0)
    up = tn(rows(n2a, n2b, n2c, n2d), rows(dpre, dpre_c, dpre_d)).astype(BF)
    down = tn(rows(act, act_c, act_d), rows(g, g_far)).astype(BF)
    for i in range(4):
        outs[i][...] = up[192 * i : 192 * i + 192, :]
        outs[4 + i][...] = down[192 * i : 192 * i + 192, :]
    line = sa[r : r + 1, :] + sb[r : r + 1, :] + sc[r : r + 1, :]
    sums[...] = jnp.broadcast_to(line, sums.shape)


def midb_kernel(mid, branch, ct, gn2, ret_a, ret_b, gain, scale, mg_out, gb_out, sums):
    step = 64
    acc = [jnp.zeros((1, mid.shape[1]), F32)] * 4
    for i in range(mid.shape[0] // step):
        at = slice(i * step, (i + 1) * step)
        ret, here = ((ret_a, i * step), (ret_b, i * step - 256))[i * step // 256]
        hat, rstd = moments(mid[at, :])
        g = gn2[at, :] + ret[here : here + step, :].astype(F32)
        mg = ct[at, :].astype(F32) + norm_back(g, hat, rstd, row(gain))
        mg_out[at, :] = mg
        gb = row(scale) * mg
        gb_out[at, :] = gb.astype(BF)
        terms = [gb, mg * branch[at, :], g * hat, g]
        acc = [a + jnp.sum(t, axis=0, keepdims=True) for a, t in zip(acc, terms)]
    sums[...] = jnp.concatenate(acc + [jnp.zeros((4, mid.shape[1]), F32)], axis=0)


def attn_bwd_kernel(
    k, q, v, lse, gb, w, wo, att, ohq, normed, up_sum, acc,
    g_first, g_last, acc_out, small_out, kt, dkacc, dvacc, do, dqs,
):
    own, kv_rows = q.shape[1], k.shape[0]
    mine = slice(HALO, HALO + own)
    g_last[192:384, :] = tn(att[...], gb[...]).astype(BF)
    do[...] = nt(gb[...], wo[...]).astype(BF)
    kt[...] = k[...].astype(F32).T.astype(BF)
    dkacc[...] = jnp.zeros(dkacc.shape, F32)
    dvacc[...] = jnp.zeros(dvacc.shape, F32)
    lane = lax.broadcasted_iota(jnp.int32, (QB, 192), 1)
    rel = jnp.zeros((192, 128), F32)
    for b in range(own // QB):
        at = slice(b * QB, b * QB + WIN)
        here = slice(b * QB, b * QB + QB)
        keys = k[at, :]
        vals = v[at, :]
        d_block = do[here, :]
        queries = jnp.concatenate([q[i, here, :] for i in range(3)], axis=0)
        zero = jnp.zeros_like(d_block)
        heads = [jnp.where((lane >= 64 * i) & (lane < 64 * i + 64), d_block, zero) for i in range(3)]
        heads = jnp.concatenate(heads, axis=0)
        p = jnp.exp(nt(keys, queries) - jnp.concatenate([lse[i : i + 1, here] for i in range(3)], axis=1))
        dp = nt(vals, heads)
        inner = jnp.sum(p * dp, axis=0, keepdims=True)
        ds = (p * (dp - inner)).astype(BF)
        dv = dvacc[at, :] + nn(p.astype(BF), heads)
        dk = dkacc[at, :] + nn(ds, queries)
        qparts = [nn(kt[64 * i : 64 * i + 64, at], ds[:, QB * i : QB * i + QB]) for i in range(3)]
        lifts = nn(kt[192:256, at], ds)
        lparts = [lifts[:, QB * i : QB * i + QB] for i in range(3)]
        dkacc[at, :] = dk
        dvacc[at, :] = dv
        dq = jnp.concatenate(qparts, axis=0) * (HEAD_DIM**-0.5)
        dqs[here, :] = dq.T.astype(BF)
        lift = jnp.concatenate(lparts, axis=0)
        high = lift.astype(BF)
        low = (lift - high.astype(F32)).astype(BF)
        rel = rel + nn(high, ohq[here, :]) + nn(low, ohq[here, :])
    dk = dkacc[:, 0:192].astype(BF)
    dv = dvacc[...].astype(BF)
    g_first[0:192, :] = tn(dqs[...], normed[mine, :]).astype(BF)
    g_first[192:384, :] = tn(dk, normed[...]).astype(BF)
    g_last[0:192, :] = tn(dv, normed[...]).astype(BF)
    for rows in (slice(0, HALO), mine, slice(HALO + own, kv_rows)):
        part = acc[rows, :] + nn(dk[rows, :], w[192:384, :]) + nn(dv[rows, :], w[384:576, :])
        acc_out[rows, :] = part + nn(dqs[...], w[0:192, :]) if rows is mine else part
    lane = lax.broadcasted_iota(jnp.int32, (16, 128), 1)
    sub = lax.broadcasted_iota(jnp.int32, (16, 128), 0)
    lane_c = lax.broadcasted_iota(jnp.int32, (24, 128), 1)
    sub_c = lax.broadcasted_iota(jnp.int32, (24, 128), 0)
    by_row, by_col = [], []
    for i in range(3):
        part = jnp.where((sub < GRID) & (lane >= 64) & (lane < 64 + GRID), rel[64 * i : 64 * i + 16, :], 0.0)
        part = pltpu.roll(part, 0, 1, stride=1, stride_axis=0)
        by_row.append(jnp.sum(part, axis=0, keepdims=True))
        keep = (sub_c >= 6) & (sub_c < 6 + GRID) & (lane_c >= 80) & (lane_c < 80 + GRID)
        part = jnp.where(keep, rel[64 * i + 8 : 64 * i + 32, :], 0.0)
        part = pltpu.roll(part, 0, 1, stride=1, stride_axis=0)
        by_col.append(jnp.sum(part, axis=0, keepdims=True))
    sums = [jnp.sum(t.astype(F32), axis=0, keepdims=True) for t in (dqs[...], dv)]
    rels = jnp.concatenate(by_row + by_col, axis=0)
    small_out[0:6, :] = jnp.concatenate([rels, jnp.zeros((6, 640), F32)], axis=1)
    none = jnp.zeros((1, 64), F32)
    small_out[6:7, :] = jnp.concatenate([sums[0], none, sums[1], none, jnp.zeros((1, 256), F32)], axis=1)
    small_out[7:8, :] = up_sum[0:1, :]


def out_kernel(mid, two, ret_a, ret_b, ct, b_down, scale_two, before, lo_out, sums):
    step = 64
    acc = [jnp.zeros((1, mid.shape[1]), F32)] * 2
    for i in range(mid.shape[0] // step):
        at = slice(i * step, (i + 1) * step)
        ret, here = ((ret_a, i * step), (ret_b, i * step - 256))[i * step // 256]
        branch_two = two[at, :] + ret[here : here + step, :].astype(F32) + row(b_down)
        lo_out[at, :] = (mid[at, :] + row(scale_two) * branch_two).astype(BF)
        up = ct[at, :].astype(F32)
        terms = [row(scale_two) * up, up * branch_two]
        acc = [a + jnp.sum(t, axis=0, keepdims=True) for a, t in zip(acc, terms)]
    sums[...] = jnp.concatenate([before[0:4, :]] + acc + [before[6:8, :]], axis=0)


def sums_kernel(left, mid, right, acc, before, sums):
    total = [jnp.zeros((1, acc.shape[1]), F32)] * 2
    at = 0
    for ref in (left, mid, right):
        for i in range(ref.shape[0] // 32):
            hat, _ = moments(ref[32 * i : 32 * i + 32, :].astype(F32))
            g = acc[at : at + 32, :]
            total = [t + jnp.sum(v, axis=0, keepdims=True) for t, v in zip(total, [g * hat, g])]
            at += 32
    sums[...] = jnp.concatenate([before[0:6, :]] + total, axis=0)


def final_kernel(x, gn1, fl, fr, mg, gain, in_out):
    step = 32
    own = x.shape[0]
    for i in range(own // step):
        at = slice(i * step, (i + 1) * step)
        hat, rstd = moments(x[at, :].astype(F32))
        g = gn1[HALO + i * step : HALO + (i + 1) * step, :]
        if (i + 1) * step <= HALO:
            g = g + fl[at, :].astype(F32)
        tail = i * step - (own - HALO)
        if tail >= 0:
            g = g + fr[tail : tail + step, :].astype(F32)
        in_out[at, :] = mg[at, :] + norm_back(g, hat, rstd, row(gain))


def unpack_kernel(sums, b_up, b_qv, rel_row, rel_col, *wholes):
    total = sums[...].astype(F32)
    b_up[...] = total[7:8, :].reshape(768)
    b_qv[...] = jnp.concatenate([total[6:7, 0:192], total[6:7, 256:448]], axis=0)
    rel_row[...] = total[0:3, 64:91]
    rel_col[...] = total[3:6, 86:113]
    for i, out in enumerate(wholes):
        out[...] = total[8 + i : 9 + i, :].reshape(768)


def op(kernel, outs, args, specs=None, out_specs=None, scratch=(), aliases=None, limit=18, after=()):
    n = len(args)

    def body(*refs):
        kernel(*refs[:n], *refs[n + len(after) :])

    return pl.pallas_call(
        body,
        out_shape=[jax.ShapeDtypeStruct(s, d) for s, d in outs],
        in_specs=(specs or [VMEM] * n) + [pl.BlockSpec(memory_space=pl.ANY)] * len(after),
        out_specs=out_specs or [VMEM] * len(outs),
        scratch_shapes=list(scratch),
        compiler_params=pltpu.CompilerParams(vmem_limit_bytes=limit * MIB),
        input_output_aliases=aliases or {},
    )(*args, *after)


VMEM = pl.BlockSpec(memory_space=pltpu.VMEM)
SMEM = pl.BlockSpec(memory_space=pltpu.SMEM)


def behind(v, first):
    if v.shape[-1] != first.shape[-1]:
        return v
    return jnp.where(first[0:1].astype(F32) > 3e38, jnp.zeros_like(v), v)


def add(*parts):
    return sum(p.astype(F32) for p in parts).astype(BF)


def halves(v, bit):
    n = v.shape[0] // 2
    return [jnp.where(bit == 0, v[:n], v[n:]), jnp.where(bit == 0, v[n:], v[:n])]


def joined(mine, other, bit):
    return jnp.concatenate([jnp.where(bit == 0, mine, other), jnp.where(bit == 0, other, mine)], axis=0)


def send(v, axis, pairs):
    return lax.ppermute(v, axis, pairs)


def make_body(ndp, nmp):
    assert nmp == 4 and ndp % 8 == 0 and ndp & (ndp - 1) == 0
    core = ("mp", [(i, i ^ 1) for i in range(nmp)])
    over_y = ("mp", [(i, i ^ 2) for i in range(nmp)])
    over_x = ("dp", [(i, i ^ 1) for i in range(ndp)])
    over_four = [("dp", [(i, i ^ b) for i in range(ndp)]) for b in (2, 1, 3)]
    over_far = [("dp", [(i, i ^ (1 << b)) for i in range(ndp)]) for b in range(2, ndp.bit_length() - 1)]
    rightward = ("mp", [(i, i + 1) for i in range(nmp - 1)])
    leftward = ("mp", [(i + 1, i) for i in range(nmp - 1)])

    def body(
        layer_in, ln1_gain, ln1_bias, w_qkv, b_qv, rel_row, rel_col, w_out, b_out, scale_attn, ln2_gain,
        ln2_bias, w_up, b_up, w_down, b_down, scale_mlp, page_lengths, patch_rows, patch_cols, cotangent,
    ):
        own, width = layer_in.shape
        kv = own + 2 * HALO
        units = w_up.shape[1]
        cols = w_qkv.shape[2]
        me = lax.axis_index("mp")
        x_bit = lax.axis_index("dp") & 1
        z_bit = (lax.axis_index("dp") >> 1) & 1
        line = ((8, width), F32)

        left, right = send(layer_in[own - HALO :], *rightward), send(layer_in[:HALO], *leftward)
        wq = jnp.transpose(w_qkv, (0, 2, 1)).reshape(3 * cols, width)
        place = lambda v, at, lane: jnp.pad(v, ((at, 8 - at - v.shape[0]), (lane, width - lane - v.shape[1])))
        small = place(rel_row, 0, 0) + place(rel_col, 3, 0) + place(b_up[None], 7, 0)
        small = small + place(b_qv[0:1], 6, 0) + place(b_qv[1:2], 6, 256)
        (packed,) = op(pack_kernel, [((3 * cols + 16, width), BF)], [wq, small])
        mine = jnp.split(halves(packed, x_bit)[0], 2, axis=0)
        packed_y = [send(v, *over_y) for v in mine]
        packed_near = send(packed, *core)
        out_y, out_near = send(w_out, *over_y), send(w_out, *core)
        up_near, down_near = send(w_up, *core), send(w_down, *core)
        normed, extk, ohq, mlp_grad = op(
            prep_kernel, [((kv, width), BF), ((kv, 64), BF), ((own, 128), BF), ((own, width), BF)],
            [
                me.reshape(1, 1), page_lengths, left, layer_in, right, ln1_gain, ln1_bias,
                patch_rows.reshape(-1, 128), patch_cols.reshape(-1, 128), cotangent, scale_mlp,
            ],
            specs=[SMEM, SMEM] + [VMEM] * 9, after=mine,
        )
        mlp_grad_y = send(mlp_grad, *over_y)

        def attention(w, after=()):
            outs = [((kv, 256), BF), ((3, own, 256), BF), ((kv, 192), BF), ((own, 192), BF), ((8, own), F32), line]
            return op(
                attn_fwd_kernel, outs, [normed, w, extk, ohq], scratch=[pltpu.VMEM((192, kv), BF)], after=after
            )

        fwd = [attention(packed)]
        packed_y = [behind(v, fwd[0][5]) for v in packed_y]
        packed_x = [send(v, *over_x) for v in packed_y]
        fwd.append(attention(packed_near, after=packed_y))
        packed_x = [behind(v, fwd[1][5]) for v in packed_x]
        packed_far = joined(jnp.concatenate(packed_y, axis=0), jnp.concatenate(packed_x, axis=0), x_bit)
        packed_diag = jnp.concatenate([send(packed_far[:304], *core), send(packed_far[304:], *core)], axis=0)
        fwd.append(attention(packed_far))
        out_far = behind(out_y, fwd[2][5])
        out_diag = send(out_far, *core)
        fwd.append(attention(packed_diag, after=[out_far]))
        ins_w, outs_w = [packed, packed_near, packed_far, packed_diag], [w_out, out_near, out_far, out_diag]
        part = ((own // 2, width), BF)
        branch, middle, n2a, n2b = op(
            mid_kernel, [((own, width), F32), ((own, width), F32), part, part],
            [*[f[3] for f in fwd], *outs_w, layer_in, b_out, scale_attn, ln2_gain, ln2_bias], after=[mlp_grad_y],
        )

        n2c, n2d = send(n2a, *over_y), send(n2b, *over_y)
        tails = [w[3 * cols :] for w in ins_w[:2]]

        def mlp(n2, g, first, dtype, after=()):
            rows = len(n2) * n2[0].shape[0]
            return op(
                functools.partial(mlp_kernel, len(n2), first),
                [((rows, units), BF)] * 4 + [((rows, width), dtype)] * 2 + [line],
                [*n2, g, w_up, w_down, up_near, down_near, *tails], after=after,
            )

        mine_mlp = mlp([n2a, n2b], mlp_grad, 0, F32)
        first_mlp = mlp([n2c], mlp_grad_y, 0, BF, after=[mine_mlp[6]])
        ret_na, ret_ba = send(first_mlp[5], *over_y), send(first_mlp[4], *over_y)
        second_mlp = mlp([n2d], mlp_grad_y, own // 2, BF, after=[first_mlp[6]])
        ret_nb, ret_bb = send(second_mlp[5], *over_y), send(second_mlp[4], *over_y)

        def weights(r, after):
            parts = [mine_mlp, first_mlp, second_mlp]
            return op(
                functools.partial(weights_kernel, r), [line] + [((width // 4, width), BF)] * 8,
                [
                    n2a, n2b, n2c, n2d, mlp_grad, mlp_grad_y, *[p[r] for p in parts], *[p[2 + r] for p in parts],
                    *[p[6] for p in parts],
                ],
                after=after,
            )

        up_far_sum, *grads_far = weights(1, [second_mlp[6], ret_na])
        mlp_near = [send(g, *core) for g in grads_far]
        up_own_sum, *grads_own = weights(0, [up_far_sum])
        up_sums = [up_own_sum, up_far_sum] + [jnp.zeros((8, width), F32)] * 2
        middle_grad, branch_grad, sums_two = op(
            midb_kernel, [((own, width), F32), ((own, width), BF), line],
            [middle, branch, cotangent, mine_mlp[5], ret_na, ret_nb, ln2_gain, scale_attn], after=[up_own_sum],
        )

        results, asked = {}, {}

        def four(v):
            mine, other = halves(v, x_bit)
            return halves(mine, z_bit) + halves(other, z_bit)

        def whole_of(own, z, x, both):
            return joined(joined(own, z, z_bit), joined(x, both, z_bit), x_bit)

        def pairs(own, z, x, both):
            return add(add(own, z).astype(F32), add(x, both).astype(F32)).astype(BF)

        def long_block(name, near):
            keep, other = yield lambda *p: halves(add(*p), x_bit), near
            there = send(other, *over_four[1])
            keep, other = yield lambda a, b: halves(add(a, b), z_bit), [keep, there]
            there = send(other, *over_four[0])
            for link in over_far:
                (keep,) = yield lambda a, b: [add(a, b)], [keep, there]
                there = send(keep, *link)
            (keep,) = yield lambda a, b: [add(a, b)], [keep, there]
            there = send(keep, *over_four[0])
            (keep,) = yield lambda a, b: [joined(a, b, z_bit)], [keep, there]
            there = send(keep, *over_four[1])
            (results[name],) = yield lambda a, b: [joined(a, b, x_bit)], [keep, there]

        def block(name, near, far=None, extra=None):
            there = [send(far, *over_y)] if far is not None else []
            keep, *others = yield lambda *p: four(add(*p)), lambda: near() + there
            there = [send(v, *link) for v, link in zip(others, over_four)]
            (keep,) = yield lambda *v: [add(*v)], [keep, *there]
            if extra:
                keep = jnp.concatenate([keep, extra[0].astype(BF)], axis=0)
            for link in over_far:
                there = send(keep, *link)
                (keep,) = yield lambda a, b: [add(a, b)], [keep, there]
            there = [send(keep, *link) for link in over_four]
            n = width // 4
            whole, *small = yield (
                lambda *v: [whole_of(*[p[:n] for p in v])] + ([pairs(*[p[n:] for p in v])] if extra else []),
                [keep, *there],
            )
            results[name] = whole
            if extra:
                flat = ((width,), F32)
                results["small"] = op(
                    unpack_kernel, [flat, ((2, 192), F32), ((3, 27), F32), ((3, 27), F32)] + [flat] * 8, small
                )

        def start(flow):
            asked[flow] = next(flow)
            return flow

        def steps(first, *flows):
            flows = [f for f in flows if f in asked]
            wanted = [(fn, args() if callable(args) else args) for fn, args in (asked.pop(f) for f in flows)]
            *given, at = lax.optimization_barrier((*[a for _, args in wanted for a in args], first))
            made, counts = [], []
            for fn, args in wanted:
                outs = fn(*[behind(a, at) for a in given[: len(args)]])
                given = given[len(args) :]
                made += outs
                counts.append(len(outs))
            outs = made = list(lax.optimization_barrier(made))
            for flow, count in zip(flows, counts):
                try:
                    asked[flow] = flow.send(outs[:count])
                except StopIteration:
                    pass
                outs = outs[count:]
            return [m for m in made if m.shape[-1] == width]

        whole = lambda parts: jnp.concatenate(parts, axis=0)
        up_flow = start(long_block("up", lambda: [whole(grads_own[:4]), whole(mlp_near[:4])]))
        down_flow = start(long_block("down", lambda: [whole(grads_own[4:]), whole(mlp_near[4:])]))
        made = steps(sums_two, up_flow, down_flow)

        grads_att, tiny, acc = [None] * 4, [None] * 4, jnp.zeros((kv, width), F32)
        n = width // 2

        def tip(arrays):
            return [arrays[-1][:16]]

        def attention_back(r, acc, after=()):
            k, q, v, att, lse, _ = fwd[r]
            *grads_att[r], acc, tiny[r] = op(
                attn_bwd_kernel, [((n, width), BF), ((n, width), BF), ((kv, width), F32), line],
                [k, q, v, lse, branch_grad, ins_w[r], outs_w[r], att, ohq, normed, up_sums[r], acc],
                scratch=[
                    pltpu.VMEM((256, kv), BF), pltpu.VMEM((kv, 256), F32), pltpu.VMEM((kv, 192), F32),
                    pltpu.VMEM((own, 192), BF), pltpu.VMEM((own, 192), BF),
                ],
                aliases={11: 2}, after=after,
            )
            return acc

        acc = attention_back(3, acc, after=tip(made))
        att_far = [send(g, *core) for g in grads_att[3]]
        made = steps(grads_att[3][0], up_flow)
        layer_out, sums_out = op(
            out_kernel, [((own, width), BF), line],
            [middle, mine_mlp[4], ret_ba, ret_bb, cotangent, b_down, scale_mlp, sums_two], after=[grads_att[3][0]],
        )
        acc = attention_back(2, acc, after=[sums_out, *tip(made)])
        made = steps(grads_att[2][0], up_flow, down_flow)
        far_sums = [add(a, behind(b, made[-1])) for a, b in zip(grads_att[2], att_far)]
        att_near, extra = [], []
        att_flow = start(block("att", lambda: [whole(grads_att[0]), whole(att_near)], whole(far_sums), extra))
        acc = attention_back(1, acc, after=tip(made) + tip(far_sums))
        att_near += [send(g, *core) for g in grads_att[1]]
        made = steps(grads_att[1][0], up_flow, down_flow)
        acc = attention_back(0, acc, after=tip(made))
        to_left, to_right = acc[:HALO].astype(BF), acc[HALO + own :].astype(BF)
        from_left, from_right = send(to_right, *rightward), send(to_left, *leftward)

        made = steps(grads_att[0][0], att_flow)

        (sums_in,) = op(sums_kernel, [line], [left, layer_in, right, acc, sums_out], after=tip(made))
        there = send(jnp.concatenate([tiny[1], sums_in, tiny[3], sums_in], axis=0), *core)
        near_small = jnp.concatenate([tiny[0], sums_in], axis=0) + there[:16]
        far_small = jnp.concatenate([tiny[2], sums_in], axis=0) + there[16:]
        extra.append(near_small + send(far_small, *over_y))
        made = steps(sums_in, up_flow, down_flow)

        (input_grad,) = op(
            final_kernel, [((own, width), F32)], [layer_in, acc, from_left, from_right, middle_grad, ln1_gain],
            after=[sums_in],
        )
        made = steps(made[-1], att_flow)
        steps(made[-1], down_flow)
        made = steps(made[-1], att_flow)
        made = steps(made[-1], up_flow, down_flow)
        while asked:
            made = steps(made[-1], *list(asked)) or made

        w_up_grad, w_down_grad = results["up"].astype(F32), results["down"].astype(F32)
        w_qkv_grad = results["att"][: 3 * cols].astype(F32)
        w_qkv_grad = jnp.transpose(w_qkv_grad.reshape(3, cols, width), (0, 2, 1))
        b_up_g, b_qv_g, rel_row_g, rel_col_g, *wholes = results["small"]
        b_out_g, scale_attn_g, ln2_gain_g, ln2_bias_g, b_down_g, scale_mlp_g, ln1_gain_g, ln1_bias_g = wholes
        return (
            layer_out, input_grad, ln1_gain_g, ln1_bias_g, w_qkv_grad, b_qv_g, rel_row_g, rel_col_g,
            results["att"][3 * cols :].astype(F32), b_out_g, scale_attn_g, ln2_gain_g, ln2_bias_g, w_up_grad, b_up_g, w_down_grad,
            b_down_g, scale_mlp_g,
        )

    return body


def solution(mesh):
    rows = P(("dp", "mp"), None)
    return jax.shard_map(
        make_body(mesh.shape["dp"], mesh.shape["mp"]),
        mesh=mesh,
        in_specs=(
            rows, P(), P(), P(None, None, "mp"), P(None, "mp"), P("mp", None), P("mp", None), P("mp", None),
            P(), P(), P(), P(), P(None, "mp"), P("mp"), P("mp", None), P(), P(), P("dp", None), P("dp"),
            P("dp"), rows,
        ),
        out_specs=(
            rows, rows, P(), P(), P(None, None, "mp"), P(None, "mp"), P("mp", None), P("mp", None),
            P("mp", None), P(), P(), P(), P(), P(None, "mp"), P("mp"), P("mp", None), P(), P(),
        ),
        check_vma=False,
    )
```

```python
import functools

import jax
import jax.numpy as jnp
import numpy as np
from jax import lax
from jax.experimental import pallas as pl
from jax.experimental.pallas import tpu as pltpu
from jax.sharding import PartitionSpec as P

HEAD_DIM = 64
GRID = 14
HALO = 160
QB = 128
WIN = QB + 2 * HALO
BIG = float(2**30)
F32 = jnp.float32
BF = jnp.bfloat16
MIB = 1024 * 1024


def nn(a, b):
    return lax.dot_general(a, b, (((1,), (0,)), ((), ())), preferred_element_type=F32)


def nt(a, b):
    return lax.dot_general(a, b, (((1,), (1,)), ((), ())), preferred_element_type=F32)


def tn(a, b):
    return lax.dot_general(a, b, (((0,), (0,)), ((), ())), preferred_element_type=F32)


def moments(v):
    centred = v - jnp.mean(v, axis=-1, keepdims=True)
    rstd = lax.rsqrt(jnp.mean(centred * centred, axis=-1, keepdims=True) + 1e-06)
    return centred * rstd, rstd


def norm_back(grad, hat, rstd, gain):
    u = grad * gain
    return rstd * (
        u - jnp.mean(u, axis=-1, keepdims=True) - hat * jnp.mean(u * hat, axis=-1, keepdims=True)
    )


def row(ref):
    return ref[...].reshape(1, ref.shape[0])


def pack_kernel(wq, small, out):
    out[0:576, :] = wq[...]
    high = small[...].astype(BF)
    low = small[...] - high.astype(F32)
    out[576:592, :] = jnp.concatenate([high.astype(F32), low], axis=0).astype(BF)


def smalls(rows):
    both = rows.astype(F32)
    return both[0:8, :] + both[8:16, :]


def prep_kernel(
    me, lengths, left, mid, right, gain, bias, rows, cols, ct, scale_two, normed, extk, ohq, g_out
):
    scale, offset = row(gain), row(bias)
    at = 0
    for ref in (left, mid, right):
        for i in range(ref.shape[0] // 32):
            hat, _ = moments(ref[32 * i : 32 * i + 32, :].astype(F32))
            normed[at : at + 32, :] = (hat * scale + offset).astype(BF)
            at += 32

    for i in range(ct.shape[0] // 64):
        here = slice(64 * i, 64 * i + 64)
        g_out[here, :] = (row(scale_two) * ct[here, :].astype(F32)).astype(BF)

    own = mid.shape[0]
    tiles = rows.shape[0]
    first = me[0, 0] * (own // 128) - 2
    pick = lambda ref: jnp.concatenate([ref[pl.ds(jnp.clip(first + t, 0, tiles - 1), 1), :] for t in range(8)], axis=1)
    by_row, by_col = pick(rows), pick(cols)
    place = lax.broadcasted_iota(jnp.int32, (1, 1024), 1) + first * 128
    inside = (place >= 0) & (place < tiles * 128)
    page = jnp.zeros((1, 1024), jnp.int32)
    end = 0
    for i in range(lengths.shape[1]):
        end = end + lengths[0, i]
        page = page + jnp.where(place >= end, 1, 0)

    def hot(sub, row_at, col_at, bit_at, swapped):
        hit = (by_row == row_at) | (by_col == col_at)
        for b in range(4):
            bit = (page >> b) & 1
            hit = hit | ((sub == bit_at + 2 * b + swapped) & (bit == 0))
            hit = hit | ((sub == bit_at + 2 * b + 1 - swapped) & (bit == 1))
        return hit

    sub = lax.broadcasted_iota(jnp.int32, (64, 1024), 0)
    rest = jnp.where(sub < 28, sub, sub - 28)
    row_at = jnp.where((rest < GRID) & (sub < 56), GRID - 1 - rest, -1)
    col_at = jnp.where((rest >= GRID) & (sub < 56), 2 * GRID - 1 - rest, -1)
    keys = hot(sub, row_at, col_at, 56, 0) | ((sub >= 56) & jnp.logical_not(inside))
    keys = jnp.where(keys, 1.0, 0.0).T
    extk[...] = keys[256 - HALO : 256 + own + HALO, :].astype(BF)
    sub = lax.broadcasted_iota(jnp.int32, (128, 1024), 0)
    none = jnp.full((128, 1024), -1, jnp.int32)
    row_at = jnp.where(sub < GRID, GRID - 1 - sub, jnp.where((sub >= 64) & (sub < 64 + GRID), sub - 64, none))
    other = sub - 16
    col_at = jnp.where((other >= 0) & (other < GRID), GRID - 1 - other, none)
    col_at = jnp.where((sub >= 80) & (sub < 80 + GRID), sub - 80, col_at)
    queries = jnp.where(hot(sub, row_at, col_at, 32, 1), 1.0, 0.0)
    ohq[...] = queries[:, 256 : 256 + own].T.astype(BF)


def bias_table(rows, cols):
    lane = lax.broadcasted_iota(jnp.int32, (16, 128), 1)
    groups = []
    for table, first in ((rows, 64), (cols, 64 + GRID)):
        table = jnp.broadcast_to(table, (16, 128))
        high = table.astype(BF).astype(F32)
        total = jnp.zeros((16, 128), F32)
        for part, at in ((high, first), (table - high, first + 2 * GRID)):
            turned = pltpu.roll(part, (at - GRID + 1) % 128, 1, stride=1, stride_axis=0)
            total = total + jnp.where((lane >= at) & (lane < at + GRID), turned, 0.0)
        groups.append(total)
    lane = lax.broadcasted_iota(jnp.int32, (96, 128), 1)
    sub = lax.broadcasted_iota(jnp.int32, (96, 128), 0)
    bits = jnp.where((sub < 8) & (lane == sub + 120), -BIG, 0.0)
    return jnp.concatenate(groups + [bits], axis=0).astype(BF)


def attn_fwd_kernel(
    normed, w, extk, ohq, k_out, q_out, v_out, att_out, lse_out, tok, vt
):
    own = mid_rows = q_out.shape[1]
    tok[...] = jnp.zeros(tok.shape, F32)
    small = smalls(w[576:592, :])
    q = nt(normed[HALO : HALO + own, :], w[0:192, :]) + small[6:7, 0:192]
    q = q.astype(BF).astype(F32) * (HEAD_DIM**-0.5)
    q = jnp.concatenate([q, jnp.zeros((own, 64), F32)], axis=1)
    lane = lax.broadcasted_iota(jnp.int32, (own, 256), 1)
    for i in range(3):
        here = (lane >= 64 * i) & (lane < 64 * i + 64)
        ext = nn(ohq[...], bias_table(small[i : i + 1, 0:128], small[3 + i : 4 + i, 0:128]))
        ext = jnp.concatenate([jnp.zeros((own, 128), F32), ext], axis=1)
        q_out[i] = (jnp.where(here, q, 0.0) + ext).astype(BF)
    k = nt(normed[...], w[192:384, :]).astype(BF)
    k_out[...] = jnp.concatenate([k, extk[...]], axis=1)
    v = nt(normed[...], w[384:576, :]) + small[6:7, 256:448]
    v_out[...] = v.astype(BF)
    vt[...] = v.T.astype(BF)
    for b in range(mid_rows // QB):
        at = slice(b * QB, b * QB + WIN)
        here = slice(b * QB, b * QB + QB)
        queries = jnp.concatenate([q_out[i, here, :] for i in range(3)], axis=0)
        scores = nt(k_out[at, :], queries)
        top = jnp.max(scores, axis=0, keepdims=True)
        e = jnp.exp(scores - top)
        total = jnp.sum(e, axis=0, keepdims=True)
        e = e.astype(BF)
        lse = top + jnp.log(total)
        parts = []
        for i in range(3):
            cols = slice(QB * i, QB * i + QB)
            parts.append(nn(vt[64 * i : 64 * i + 64, at], e[:, cols]) / total[:, cols])
            lse_out[i : i + 1, here] = lse[:, cols]
        att_out[here, :] = jnp.concatenate(parts, axis=0).T.astype(BF)


def mid_kernel(
    a0, a1, a2, a3, w0, w1, w2, w3, x, b_out, scale, gain, bias, branch_out, mid_out, n2_first, n2_second
):
    step = 128
    for i in range(x.shape[0] // step):
        at = slice(i * step, (i + 1) * step)
        branch = nn(a0[at, :], w0[...]) + nn(a1[at, :], w1[...])
        branch = branch + nn(a2[at, :], w2[...]) + nn(a3[at, :], w3[...])
        branch = branch + row(b_out)
        middle = x[at, :].astype(F32) + row(scale) * branch
        hat, _ = moments(middle)
        branch_out[at, :] = branch
        mid_out[at, :] = middle
        out = (n2_first, n2_second)[i // 2]
        here = i % 2 * step
        out[here : here + step, :] = (hat * row(gain) + row(bias)).astype(BF)


def mlp_kernel(chunks, first, *refs):
    n2 = refs[:chunks]
    g, wu0, wd0, wu1, wd1, s0, s1, act0, act1, dpre0, dpre1, b_out, n_out, sums = refs[chunks:]
    c = 0.7978845608028654
    step = 256
    totals = []
    for wu, wd, s, act, dpre, r in ((wu0, wd0, s0, act0, dpre0, 0), (wu1, wd1, s1, act1, dpre1, 1)):
        bias = smalls(s[...])[7:8, :]
        total = jnp.zeros((1, wu.shape[1]), F32)
        for i in range(chunks):
            at = slice(i * step, (i + 1) * step)
            pre = nn(n2[i][...], wu[...]) + bias
            sq = pre * pre
            t = jnp.tanh(c * pre * (1.0 + 0.044715 * sq))
            half = 0.5 * (1.0 + t)
            slope = half + (0.5 * c) * pre * (1.0 - t * t) * (1.0 + (3 * 0.044715) * sq)
            a = (pre * half).astype(BF)
            act[at, :] = a
            dp = (nt(g[first + i * step : first + (i + 1) * step, :], wd[...]) * slope).astype(BF)
            dpre[at, :] = dp
            total = total + jnp.sum(dp.astype(F32), axis=0, keepdims=True)
        totals.append(total)
    for i in range(chunks):
        at = slice(i * step, (i + 1) * step)
        n_out[at, :] = (nt(dpre0[at, :], wu0[...]) + nt(dpre1[at, :], wu1[...])).astype(n_out.dtype)
        b_out[at, :] = (nn(act0[at, :], wd0[...]) + nn(act1[at, :], wd1[...])).astype(b_out.dtype)
    sums[...] = jnp.concatenate(totals + [jnp.zeros((6, 768), F32)], axis=0)


def weights_kernel(
    r, n2a, n2b, n2c, n2d, g, g_far, act, act_c, act_d, dpre, dpre_c, dpre_d, sa, sb, sc, sums, *outs
):
    rows = lambda *parts: jnp.concatenate([p[...] for p in parts], axis=0)
    up = tn(rows(n2a, n2b, n2c, n2d), rows(dpre, dpre_c, dpre_d)).astype(BF)
    down = tn(rows(act, act_c, act_d), rows(g, g_far)).astype(BF)
    for i in range(4):
        outs[i][...] = up[192 * i : 192 * i + 192, :]
        outs[4 + i][...] = down[192 * i : 192 * i + 192, :]
    line = sa[r : r + 1, :] + sb[r : r + 1, :] + sc[r : r + 1, :]
    sums[...] = jnp.broadcast_to(line, sums.shape)


def midb_kernel(mid, branch, ct, gn2, ret_a, ret_b, gain, scale, mg_out, gb_out, sums):
    step = 64
    acc = [jnp.zeros((1, mid.shape[1]), F32)] * 4
    for i in range(mid.shape[0] // step):
        at = slice(i * step, (i + 1) * step)
        ret, here = ((ret_a, i * step), (ret_b, i * step - 256))[i * step // 256]
        hat, rstd = moments(mid[at, :])
        g = gn2[at, :] + ret[here : here + step, :].astype(F32)
        mg = ct[at, :].astype(F32) + norm_back(g, hat, rstd, row(gain))
        mg_out[at, :] = mg
        gb = row(scale) * mg
        gb_out[at, :] = gb.astype(BF)
        terms = [gb, mg * branch[at, :], g * hat, g]
        acc = [a + jnp.sum(t, axis=0, keepdims=True) for a, t in zip(acc, terms)]
    sums[...] = jnp.concatenate(acc + [jnp.zeros((4, mid.shape[1]), F32)], axis=0)


def attn_bwd_kernel(
    k, q, v, lse, gb, w, wo, att, ohq, normed, up_sum, acc,
    g_first, g_last, acc_out, small_out, kt, dkacc, dvacc, do, dqs,
):
    own, kv_rows = q.shape[1], k.shape[0]
    mine = slice(HALO, HALO + own)
    g_last[192:384, :] = tn(att[...], gb[...]).astype(BF)
    do[...] = nt(gb[...], wo[...]).astype(BF)
    kt[...] = k[...].astype(F32).T.astype(BF)
    dkacc[...] = jnp.zeros(dkacc.shape, F32)
    dvacc[...] = jnp.zeros(dvacc.shape, F32)
    lane = lax.broadcasted_iota(jnp.int32, (QB, 192), 1)
    rel = jnp.zeros((192, 128), F32)
    for b in range(own // QB):
        at = slice(b * QB, b * QB + WIN)
        here = slice(b * QB, b * QB + QB)
        keys = k[at, :]
        vals = v[at, :]
        d_block = do[here, :]
        queries = jnp.concatenate([q[i, here, :] for i in range(3)], axis=0)
        zero = jnp.zeros_like(d_block)
        heads = [jnp.where((lane >= 64 * i) & (lane < 64 * i + 64), d_block, zero) for i in range(3)]
        heads = jnp.concatenate(heads, axis=0)
        p = jnp.exp(nt(keys, queries) - jnp.concatenate([lse[i : i + 1, here] for i in range(3)], axis=1))
        dp = nt(vals, heads)
        inner = jnp.sum(p * dp, axis=0, keepdims=True)
        ds = (p * (dp - inner)).astype(BF)
        dv = dvacc[at, :] + nn(p.astype(BF), heads)
        dk = dkacc[at, :] + nn(ds, queries)
        qparts = [nn(kt[64 * i : 64 * i + 64, at], ds[:, QB * i : QB * i + QB]) for i in range(3)]
        lifts = nn(kt[192:256, at], ds)
        lparts = [lifts[:, QB * i : QB * i + QB] for i in range(3)]
        dkacc[at, :] = dk
        dvacc[at, :] = dv
        dq = jnp.concatenate(qparts, axis=0) * (HEAD_DIM**-0.5)
        dqs[here, :] = dq.T.astype(BF)
        lift = jnp.concatenate(lparts, axis=0)
        high = lift.astype(BF)
        low = (lift - high.astype(F32)).astype(BF)
        rel = rel + nn(high, ohq[here, :]) + nn(low, ohq[here, :])
    dk = dkacc[:, 0:192].astype(BF)
    dv = dvacc[...].astype(BF)
    g_first[0:192, :] = tn(dqs[...], normed[mine, :]).astype(BF)
    g_first[192:384, :] = tn(dk, normed[...]).astype(BF)
    g_last[0:192, :] = tn(dv, normed[...]).astype(BF)
    for rows in (slice(0, HALO), mine, slice(HALO + own, kv_rows)):
        part = acc[rows, :] + nn(dk[rows, :], w[192:384, :]) + nn(dv[rows, :], w[384:576, :])
        acc_out[rows, :] = part + nn(dqs[...], w[0:192, :]) if rows is mine else part
    lane = lax.broadcasted_iota(jnp.int32, (16, 128), 1)
    sub = lax.broadcasted_iota(jnp.int32, (16, 128), 0)
    lane_c = lax.broadcasted_iota(jnp.int32, (24, 128), 1)
    sub_c = lax.broadcasted_iota(jnp.int32, (24, 128), 0)
    by_row, by_col = [], []
    for i in range(3):
        part = jnp.where((sub < GRID) & (lane >= 64) & (lane < 64 + GRID), rel[64 * i : 64 * i + 16, :], 0.0)
        part = pltpu.roll(part, 0, 1, stride=1, stride_axis=0)
        by_row.append(jnp.sum(part, axis=0, keepdims=True))
        keep = (sub_c >= 6) & (sub_c < 6 + GRID) & (lane_c >= 80) & (lane_c < 80 + GRID)
        part = jnp.where(keep, rel[64 * i + 8 : 64 * i + 32, :], 0.0)
        part = pltpu.roll(part, 0, 1, stride=1, stride_axis=0)
        by_col.append(jnp.sum(part, axis=0, keepdims=True))
    sums = [jnp.sum(t.astype(F32), axis=0, keepdims=True) for t in (dqs[...], dv)]
    rels = jnp.concatenate(by_row + by_col, axis=0)
    small_out[0:6, :] = jnp.concatenate([rels, jnp.zeros((6, 640), F32)], axis=1)
    none = jnp.zeros((1, 64), F32)
    small_out[6:7, :] = jnp.concatenate([sums[0], none, sums[1], none, jnp.zeros((1, 256), F32)], axis=1)
    small_out[7:8, :] = up_sum[0:1, :]


def out_kernel(mid, two, ret_a, ret_b, ct, b_down, scale_two, before, lo_out, sums):
    step = 64
    acc = [jnp.zeros((1, mid.shape[1]), F32)] * 2
    for i in range(mid.shape[0] // step):
        at = slice(i * step, (i + 1) * step)
        ret, here = ((ret_a, i * step), (ret_b, i * step - 256))[i * step // 256]
        branch_two = two[at, :] + ret[here : here + step, :].astype(F32) + row(b_down)
        lo_out[at, :] = (mid[at, :] + row(scale_two) * branch_two).astype(BF)
        up = ct[at, :].astype(F32)
        terms = [row(scale_two) * up, up * branch_two]
        acc = [a + jnp.sum(t, axis=0, keepdims=True) for a, t in zip(acc, terms)]
    sums[...] = jnp.concatenate([before[0:4, :]] + acc + [before[6:8, :]], axis=0)


def sums_kernel(left, mid, right, acc, before, sums):
    total = [jnp.zeros((1, acc.shape[1]), F32)] * 2
    at = 0
    for ref in (left, mid, right):
        for i in range(ref.shape[0] // 32):
            hat, _ = moments(ref[32 * i : 32 * i + 32, :].astype(F32))
            g = acc[at : at + 32, :]
            total = [t + jnp.sum(v, axis=0, keepdims=True) for t, v in zip(total, [g * hat, g])]
            at += 32
    sums[...] = jnp.concatenate([before[0:6, :]] + total, axis=0)


def final_kernel(x, gn1, fl, fr, mg, gain, in_out):
    step = 32
    own = x.shape[0]
    for i in range(own // step):
        at = slice(i * step, (i + 1) * step)
        hat, rstd = moments(x[at, :].astype(F32))
        g = gn1[HALO + i * step : HALO + (i + 1) * step, :]
        if (i + 1) * step <= HALO:
            g = g + fl[at, :].astype(F32)
        tail = i * step - (own - HALO)
        if tail >= 0:
            g = g + fr[tail : tail + step, :].astype(F32)
        in_out[at, :] = mg[at, :] + norm_back(g, hat, rstd, row(gain))


def unpack_kernel(sums, b_up, b_qv, rel_row, rel_col, *wholes):
    total = sums[...].astype(F32)
    b_up[...] = total[7:8, :].reshape(768)
    b_qv[...] = jnp.concatenate([total[6:7, 0:192], total[6:7, 256:448]], axis=0)
    rel_row[...] = total[0:3, 64:91]
    rel_col[...] = total[3:6, 86:113]
    for i, out in enumerate(wholes):
        out[...] = total[8 + i : 9 + i, :].reshape(768)


def op(kernel, outs, args, specs=None, out_specs=None, scratch=(), aliases=None, limit=18, after=()):
    n = len(args)

    def body(*refs):
        kernel(*refs[:n], *refs[n + len(after) :])

    return pl.pallas_call(
        body,
        out_shape=[jax.ShapeDtypeStruct(s, d) for s, d in outs],
        in_specs=(specs or [VMEM] * n) + [pl.BlockSpec(memory_space=pl.ANY)] * len(after),
        out_specs=out_specs or [VMEM] * len(outs),
        scratch_shapes=list(scratch),
        compiler_params=pltpu.CompilerParams(vmem_limit_bytes=limit * MIB),
        input_output_aliases=aliases or {},
    )(*args, *after)


VMEM = pl.BlockSpec(memory_space=pltpu.VMEM)
SMEM = pl.BlockSpec(memory_space=pltpu.SMEM)


def behind(v, first):
    if v.shape[-1] != first.shape[-1]:
        return v
    return jnp.where(first[0:1].astype(F32) > 3e38, jnp.zeros_like(v), v)


def add(*parts):
    return sum(p.astype(F32) for p in parts).astype(BF)


def halves(v, bit):
    n = v.shape[0] // 2
    return [jnp.where(bit == 0, v[:n], v[n:]), jnp.where(bit == 0, v[n:], v[:n])]


def joined(mine, other, bit):
    return jnp.concatenate([jnp.where(bit == 0, mine, other), jnp.where(bit == 0, other, mine)], axis=0)


def send(v, axis, pairs):
    return lax.ppermute(v, axis, pairs)


def make_body(ndp, nmp):
    assert nmp == 4 and ndp % 8 == 0 and ndp & (ndp - 1) == 0
    core = ("mp", [(i, i ^ 1) for i in range(nmp)])
    over_y = ("mp", [(i, i ^ 2) for i in range(nmp)])
    over_x = ("dp", [(i, i ^ 1) for i in range(ndp)])
    over_four = [("dp", [(i, i ^ b) for i in range(ndp)]) for b in (2, 1, 3)]
    over_far = [("dp", [(i, i ^ (1 << b)) for i in range(ndp)]) for b in range(2, ndp.bit_length() - 1)]
    rightward = ("mp", [(i, i + 1) for i in range(nmp - 1)])
    leftward = ("mp", [(i + 1, i) for i in range(nmp - 1)])

    def body(
        layer_in, ln1_gain, ln1_bias, w_qkv, b_qv, rel_row, rel_col, w_out, b_out, scale_attn, ln2_gain,
        ln2_bias, w_up, b_up, w_down, b_down, scale_mlp, page_lengths, patch_rows, patch_cols, cotangent,
    ):
        own, width = layer_in.shape
        kv = own + 2 * HALO
        units = w_up.shape[1]
        cols = w_qkv.shape[2]
        me = lax.axis_index("mp")
        x_bit = lax.axis_index("dp") & 1
        z_bit = (lax.axis_index("dp") >> 1) & 1
        line = ((8, width), F32)

        left, right = send(layer_in[own - HALO :], *rightward), send(layer_in[:HALO], *leftward)
        wq = jnp.transpose(w_qkv, (0, 2, 1)).reshape(3 * cols, width)
        place = lambda v, at, lane: jnp.pad(v, ((at, 8 - at - v.shape[0]), (lane, width - lane - v.shape[1])))
        small = place(rel_row, 0, 0) + place(rel_col, 3, 0) + place(b_up[None], 7, 0)
        small = small + place(b_qv[0:1], 6, 0) + place(b_qv[1:2], 6, 256)
        (packed,) = op(pack_kernel, [((3 * cols + 16, width), BF)], [wq, small])
        mine = jnp.split(halves(packed, x_bit)[0], 2, axis=0)
        packed_y = [send(v, *over_y) for v in mine]
        packed_near = send(packed, *core)
        out_y, out_near = send(w_out, *over_y), send(w_out, *core)
        up_near, down_near = send(w_up, *core), send(w_down, *core)
        normed, extk, ohq, mlp_grad = op(
            prep_kernel, [((kv, width), BF), ((kv, 64), BF), ((own, 128), BF), ((own, width), BF)],
            [
                me.reshape(1, 1), page_lengths, left, layer_in, right, ln1_gain, ln1_bias,
                patch_rows.reshape(-1, 128), patch_cols.reshape(-1, 128), cotangent, scale_mlp,
            ],
            specs=[SMEM, SMEM] + [VMEM] * 9, after=mine,
        )
        mlp_grad_y = send(mlp_grad, *over_y)

        def attention(w, after=()):
            outs = [((kv, 256), BF), ((3, own, 256), BF), ((kv, 192), BF), ((own, 192), BF), ((8, own), F32), line]
            return op(
                attn_fwd_kernel, outs, [normed, w, extk, ohq], scratch=[pltpu.VMEM((192, kv), BF)], after=after
            )

        fwd = [attention(packed)]
        packed_y = [behind(v, fwd[0][5]) for v in packed_y]
        packed_x = [send(v, *over_x) for v in packed_y]
        fwd.append(attention(packed_near, after=packed_y))
        packed_x = [behind(v, fwd[1][5]) for v in packed_x]
        packed_far = joined(jnp.concatenate(packed_y, axis=0), jnp.concatenate(packed_x, axis=0), x_bit)
        packed_diag = jnp.concatenate([send(packed_far[:304], *core), send(packed_far[304:], *core)], axis=0)
        fwd.append(attention(packed_far))
        out_far = behind(out_y, fwd[2][5])
        out_diag = send(out_far, *core)
        fwd.append(attention(packed_diag, after=[out_far]))
        ins_w, outs_w = [packed, packed_near, packed_far, packed_diag], [w_out, out_near, out_far, out_diag]
        part = ((own // 2, width), BF)
        branch, middle, n2a, n2b = op(
            mid_kernel, [((own, width), F32), ((own, width), F32), part, part],
            [*[f[3] for f in fwd], *outs_w, layer_in, b_out, scale_attn, ln2_gain, ln2_bias], after=[mlp_grad_y],
        )

        n2c, n2d = send(n2a, *over_y), send(n2b, *over_y)
        tails = [w[3 * cols :] for w in ins_w[:2]]

        def mlp(n2, g, first, dtype, after=()):
            rows = len(n2) * n2[0].shape[0]
            return op(
                functools.partial(mlp_kernel, len(n2), first),
                [((rows, units), BF)] * 4 + [((rows, width), dtype)] * 2 + [line],
                [*n2, g, w_up, w_down, up_near, down_near, *tails], after=after,
            )

        mine_mlp = mlp([n2a, n2b], mlp_grad, 0, F32)
        first_mlp = mlp([n2c], mlp_grad_y, 0, BF, after=[mine_mlp[6]])
        ret_na, ret_ba = send(first_mlp[5], *over_y), send(first_mlp[4], *over_y)
        second_mlp = mlp([n2d], mlp_grad_y, own // 2, BF, after=[first_mlp[6]])
        ret_nb, ret_bb = send(second_mlp[5], *over_y), send(second_mlp[4], *over_y)

        def weights(r, after):
            parts = [mine_mlp, first_mlp, second_mlp]
            return op(
                functools.partial(weights_kernel, r), [line] + [((width // 4, width), BF)] * 8,
                [
                    n2a, n2b, n2c, n2d, mlp_grad, mlp_grad_y, *[p[r] for p in parts], *[p[2 + r] for p in parts],
                    *[p[6] for p in parts],
                ],
                after=after,
            )

        up_far_sum, *grads_far = weights(1, [second_mlp[6], ret_na])
        mlp_near = [send(g, *core) for g in grads_far]
        up_own_sum, *grads_own = weights(0, [up_far_sum])
        up_sums = [up_own_sum, up_far_sum] + [jnp.zeros((8, width), F32)] * 2
        middle_grad, branch_grad, sums_two = op(
            midb_kernel, [((own, width), F32), ((own, width), BF), line],
            [middle, branch, cotangent, mine_mlp[5], ret_na, ret_nb, ln2_gain, scale_attn], after=[up_own_sum],
        )

        results, asked = {}, {}

        def four(v):
            mine, other = halves(v, x_bit)
            return halves(mine, z_bit) + halves(other, z_bit)

        def whole_of(own, z, x, both):
            return joined(joined(own, z, z_bit), joined(x, both, z_bit), x_bit)

        def pairs(own, z, x, both):
            return add(add(own, z).astype(F32), add(x, both).astype(F32)).astype(BF)

        def long_block(name, near):
            keep, other = yield lambda *p: halves(add(*p), x_bit), near
            there = send(other, *over_four[1])
            keep, other = yield lambda a, b: halves(add(a, b), z_bit), [keep, there]
            there = send(other, *over_four[0])
            for link in over_far:
                (keep,) = yield lambda a, b: [add(a, b)], [keep, there]
                there = send(keep, *link)
            (keep,) = yield lambda a, b: [add(a, b)], [keep, there]
            there = send(keep, *over_four[0])
            (keep,) = yield lambda a, b: [joined(a, b, z_bit)], [keep, there]
            there = send(keep, *over_four[1])
            (results[name],) = yield lambda a, b: [joined(a, b, x_bit)], [keep, there]

        def block(name, near, far=None, extra=None):
            there = [send(far, *over_y)] if far is not None else []
            keep, *others = yield lambda *p: four(add(*p)), lambda: near() + there
            there = [send(v, *link) for v, link in list(zip(others, over_four))[::-1]][::-1]
            (keep,) = yield lambda *v: [add(*v)], [keep, *there]
            if extra:
                keep = jnp.concatenate([keep, extra[0].astype(BF)], axis=0)
            for link in over_far:
                there = send(keep, *link)
                (keep,) = yield lambda a, b: [add(a, b)], [keep, there]
            there = [send(keep, *link) for link in over_four[::-1]][::-1]
            n = width // 4
            whole, *small = yield (
                lambda *v: [whole_of(*[p[:n] for p in v])] + ([pairs(*[p[n:] for p in v])] if extra else []),
                [keep, *there],
            )
            results[name] = whole
            if extra:
                flat = ((width,), F32)
                results["small"] = op(
                    unpack_kernel, [flat, ((2, 192), F32), ((3, 27), F32), ((3, 27), F32)] + [flat] * 8, small
                )

        def start(flow):
            asked[flow] = next(flow)
            return flow

        def steps(first, *flows):
            flows = [f for f in flows if f in asked]
            wanted = [(fn, args() if callable(args) else args) for fn, args in (asked.pop(f) for f in flows)]
            *given, at = lax.optimization_barrier((*[a for _, args in wanted for a in args], first))
            made, counts = [], []
            for fn, args in wanted:
                outs = fn(*[behind(a, at) for a in given[: len(args)]])
                given = given[len(args) :]
                made += outs
                counts.append(len(outs))
            outs = made = list(lax.optimization_barrier(made))
            for flow, count in zip(flows, counts):
                try:
                    asked[flow] = flow.send(outs[:count])
                except StopIteration:
                    pass
                outs = outs[count:]
            return [m for m in made if m.shape[-1] == width]

        whole = lambda parts: jnp.concatenate(parts, axis=0)
        up_flow = start(long_block("up", lambda: [whole(grads_own[:4]), whole(mlp_near[:4])]))
        down_flow = start(long_block("down", lambda: [whole(grads_own[4:]), whole(mlp_near[4:])]))
        made = steps(sums_two, up_flow, down_flow)

        grads_att, tiny, acc = [None] * 4, [None] * 4, jnp.zeros((kv, width), F32)
        n = width // 2

        def tip(arrays):
            return [arrays[-1][:16]]

        def attention_back(r, acc, after=()):
            k, q, v, att, lse, _ = fwd[r]
            *grads_att[r], acc, tiny[r] = op(
                attn_bwd_kernel, [((n, width), BF), ((n, width), BF), ((kv, width), F32), line],
                [k, q, v, lse, branch_grad, ins_w[r], outs_w[r], att, ohq, normed, up_sums[r], acc],
                scratch=[
                    pltpu.VMEM((256, kv), BF), pltpu.VMEM((kv, 256), F32), pltpu.VMEM((kv, 192), F32),
                    pltpu.VMEM((own, 192), BF), pltpu.VMEM((own, 192), BF),
                ],
                aliases={11: 2}, after=after,
            )
            return acc

        acc = attention_back(3, acc, after=tip(made))
        att_far = [send(g, *core) for g in grads_att[3]]
        made = steps(grads_att[3][0], up_flow)
        layer_out, sums_out = op(
            out_kernel, [((own, width), BF), line],
            [middle, mine_mlp[4], ret_ba, ret_bb, cotangent, b_down, scale_mlp, sums_two], after=[grads_att[3][0]],
        )
        acc = attention_back(2, acc, after=[sums_out, *tip(made)])
        made = steps(grads_att[2][0], up_flow, down_flow)
        far_sums = [add(a, behind(b, made[-1])) for a, b in zip(grads_att[2], att_far)]
        att_near, extra = [], []
        att_flow = start(block("att", lambda: [whole(grads_att[0]), whole(att_near)], whole(far_sums), extra))
        acc = attention_back(1, acc, after=tip(made) + tip(far_sums))
        att_near += [send(g, *core) for g in grads_att[1]]
        made = steps(grads_att[1][0], up_flow, down_flow)
        acc = attention_back(0, acc, after=tip(made))
        to_left, to_right = acc[:HALO].astype(BF), acc[HALO + own :].astype(BF)
        from_left, from_right = send(to_right, *rightward), send(to_left, *leftward)

        made = steps(grads_att[0][0], att_flow)

        (sums_in,) = op(sums_kernel, [line], [left, layer_in, right, acc, sums_out], after=tip(made))
        there = send(jnp.concatenate([tiny[1], sums_in, tiny[3], sums_in], axis=0), *core)
        near_small = jnp.concatenate([tiny[0], sums_in], axis=0) + there[:16]
        far_small = jnp.concatenate([tiny[2], sums_in], axis=0) + there[16:]
        extra.append(near_small + send(far_small, *over_y))
        made = steps(sums_in, up_flow, down_flow)

        (input_grad,) = op(
            final_kernel, [((own, width), F32)], [layer_in, acc, from_left, from_right, middle_grad, ln1_gain],
            after=[sums_in],
        )
        made = steps(made[-1], att_flow)
        steps(made[-1], down_flow)
        made = steps(made[-1], att_flow)
        made = steps(made[-1], up_flow, down_flow)
        while asked:
            made = steps(made[-1], *list(asked)) or made

        w_up_grad, w_down_grad = results["up"].astype(F32), results["down"].astype(F32)
        w_qkv_grad = results["att"][: 3 * cols].astype(F32)
        w_qkv_grad = jnp.transpose(w_qkv_grad.reshape(3, cols, width), (0, 2, 1))
        b_up_g, b_qv_g, rel_row_g, rel_col_g, *wholes = results["small"]
        b_out_g, scale_attn_g, ln2_gain_g, ln2_bias_g, b_down_g, scale_mlp_g, ln1_gain_g, ln1_bias_g = wholes
        return (
            layer_out, input_grad, ln1_gain_g, ln1_bias_g, w_qkv_grad, b_qv_g, rel_row_g, rel_col_g,
            results["att"][3 * cols :].astype(F32), b_out_g, scale_attn_g, ln2_gain_g, ln2_bias_g, w_up_grad, b_up_g, w_down_grad,
            b_down_g, scale_mlp_g,
        )

    return body


def solution(mesh):
    rows = P(("dp", "mp"), None)
    return jax.shard_map(
        make_body(mesh.shape["dp"], mesh.shape["mp"]),
        mesh=mesh,
        in_specs=(
            rows, P(), P(), P(None, None, "mp"), P(None, "mp"), P("mp", None), P("mp", None), P("mp", None),
            P(), P(), P(), P(), P(None, "mp"), P("mp"), P("mp", None), P(), P(), P("dp", None), P("dp"),
            P("dp"), rows,
        ),
        out_specs=(
            rows, rows, P(), P(), P(None, None, "mp"), P(None, "mp"), P("mp", None), P("mp", None),
            P("mp", None), P(), P(), P(), P(), P(None, "mp"), P("mp"), P("mp", None), P(), P(),
        ),
        check_vma=False,
    )
```
